32 devices in a mesh: grp: 4 (over x, core), wide: 8 (over z, y).
Axes of the slice: x: 2, y: 2, z: 4, core: 2. Of those that a mesh axis runs over, the one named last changes fastest.
Arguments:
- tokens: bfloat16 [8192, 2048], P(('grp', 'wide')), may hold values from -6 to 6
- lengths: int32 [32], P(('grp', 'wide')), may hold values from 1 to 256, 6144 in all
- cotangent: bfloat16 [8192, 2048], P(('grp', 'wide')), may hold values from -6 to 6
- norm_gain: float32 [2048], P(('grp', 'wide')), may hold values from 0.25 to 1.75
- conv_weight: float32 [2048, 3], P(('grp', 'wide')), may hold values from -3.5 to 3.5
- w_query: float32 [2048, 256], P(('grp', 'wide')), may hold values from -0.125 to 0.125
- w_key: float32 [2048, 256], P(('grp', 'wide')), may hold values from -0.125 to 0.125
- w_value: float32 [2048, 2048], P(('grp', 'wide')), may hold values from -0.125 to 0.125
- w_query_window: float32 [2048, 2048], P(('grp', 'wide')), may hold values from -0.125 to 0.125
- w_key_window: float32 [2048, 2048], P(('grp', 'wide')), may hold values from -0.125 to 0.125
- w_out: float32 [2048, 2048], P(('grp', 'wide')), may hold values from -0.375 to 0.375
- ffn_gain: float32 [2048], P(('grp', 'wide')), may hold values from 0.25 to 1.75
- w_gate: float32 [2048, 5504], P(('grp', 'wide')), may hold values from -0.125 to 0.125
- w_up: float32 [2048, 5504], P(('grp', 'wide')), may hold values from -0.125 to 0.125
- w_down: float32 [5504, 2048], P(('grp', 'wide')), may hold values from -0.078125 to 0.078125
Outputs:
- block_out: bfloat16 [8192, 2048], P(('grp', 'wide'))
- grad_tokens: bfloat16 [8192, 2048], P(('grp', 'wide'))
- grad_norm_gain: float32 [2048], P(('grp', 'wide'))
- grad_conv: float32 [2048, 3], P(('grp', 'wide'))
- grad_query: float32 [2048, 256], P(('grp', 'wide'))
- grad_key: float32 [2048, 256], P(('grp', 'wide'))
- grad_value: float32 [2048, 2048], P(('grp', 'wide'))
- grad_query_window: float32 [2048, 2048], P(('grp', 'wide'))
- grad_key_window: float32 [2048, 2048], P(('grp', 'wide'))
- grad_out: float32 [2048, 2048], P(('grp', 'wide'))
- grad_ffn_gain: float32 [2048], P(('grp', 'wide'))
- grad_gate: float32 [2048, 5504], P(('grp', 'wide'))
- grad_up: float32 [2048, 5504], P(('grp', 'wide'))
- grad_down: float32 [5504, 2048], P(('grp', 'wide'))
The draws below stay inside these ranges and needn't reach their ends.
Inputs may be any that keep to these rules, and one draw needn't show every extreme that they name: lengths[b] is the number of real tokens in slot b; at least one slot is full with 256.
All inputs are finite; a program needn't handle non-finite values. No bound on the sum of `lengths` on one device may be relied on, other than what follows from the above.
Results may differ from the reference program's by a relative error of at most 0.017.
The reference program's roundings to bfloat16 on the way count: a program that leaves them out, or rounds other values in their place, can miss the bound.
Values may be sent and summed in bfloat16 or wider, within the bound.
No kernel may reach another device: no remote copies, remote signals or barrier semaphores. Data moves between devices by JAX's collectives and lax.ppermute only.
A program may use at most 384 MiB of HBM per device.

```python
import math
import jax
import jax.numpy as jnp
import numpy as np
from jax import lax

D = 2048
FF = 5504
HEADS = 16
FEAT = 16
WINDOW = 64
CONV_K = 3
TOK_DEV = 256
VHEAD = 128
TOKENS = 8192
DEVICES = 32


def level_of(rng, extent, shards, smallest, largest):
    loudness, own = 1.0, jax.random.fold_in(rng, 6)
    for dim, shards_of in shards:
        steps = jnp.exp(jax.random.uniform(jax.random.fold_in(own, dim), (shards_of,), jnp.float32, smallest / len(shards), largest / len(shards)))
        loudness = loudness * jnp.repeat(steps, extent[dim] // shards_of).reshape([-1 if axis == dim else 1 for axis in range(len(extent))])
    return loudness


def profile(count, total, bound, skew):
    portions = [(1 << 20) // math.isqrt(standing ** skew) + 1 for standing in range(2, count + 1)]
    surplus, holding = total - bound - (count - 1), [1] * (count - 1)
    while surplus > 0:
        free = [i for i in range(count - 1) if holding[i] < bound]
        whole, left = sum([portions[i] for i in free]), surplus
        for i in free:
            addition = min(bound - holding[i], max(1, left * portions[i] // whole), surplus)
            holding[i] = holding[i] + addition
            surplus = surplus - addition
    return np.array([bound] + holding)


def ragged(stream_key, number_of, total, limit, lean):
    if number_of == 2:
        one = jax.random.randint(stream_key, (), max(1, total - limit), min(limit, total - 1) + 1)
        return jnp.stack([one, total - one])
    tallies = jnp.asarray(profile(number_of, total, limit, lean), jnp.int32)
    twos = (number_of - 1) // 2
    giver, receiver = tallies[1:1 + 2 * twos:2], tallies[2:2 + 2 * twos:2]
    slack = jnp.minimum(giver - 1, limit - receiver)
    passed = jax.random.randint(jax.random.fold_in(stream_key, 1), (twos,), 0, 1 << 20) % (slack + 1)
    tallies = tallies.at[1:1 + 2 * twos:2].set(giver - passed).at[2:2 + 2 * twos:2].set(receiver + passed)
    return tallies[jax.random.permutation(jax.random.fold_in(stream_key, 2), number_of)]


def noise(stream_key, extent, spread, most, pieces=(), held_as=jnp.bfloat16):
    array = spread * jax.random.normal(stream_key, extent, jnp.float32)
    if pieces:
        array = array * level_of(stream_key, extent, pieces, -0.22, 0.18)
    return jnp.clip(array, -most, most).astype(held_as)


def setup_inputs(seed: int = 0) -> dict:
    splits = jax.random.split(jax.random.key(seed), 16)
    return {
        "tokens": noise(splits[0], (TOKENS, D), 1.0, 6.0, ((0, 32),)),
        "lengths": ragged(splits[1], DEVICES, DEVICES * TOK_DEV * 3 // 4, TOK_DEV, 1).astype(jnp.int32),
        "cotangent": noise(splits[2], (TOKENS, D), 1.0, 6.0, ((0, 32),)),
        "norm_gain": jnp.clip(1.0 + 0.15 * jax.random.normal(splits[3], (D,), jnp.float32), 0.25, 1.75),
        "conv_weight": noise(splits[4], (D, CONV_K), CONV_K ** -0.5, 3.5, ((0, 32),), jnp.float32),
        "w_query": noise(splits[5], (D, HEADS * FEAT), D ** -0.5, 0.125, ((0, 32),), jnp.float32),
        "w_key": noise(splits[6], (D, HEADS * FEAT), D ** -0.5, 0.125, ((0, 32),), jnp.float32),
        "w_value": noise(splits[7], (D, D), D ** -0.5, 0.125, ((0, 32),), jnp.float32),
        "w_query_window": noise(splits[8], (D, D), D ** -0.5, 0.125, ((0, 32),), jnp.float32),
        "w_key_window": noise(splits[9], (D, D), D ** -0.5, 0.125, ((0, 32),), jnp.float32),
        "w_out": noise(splits[10], (D, D), (D // 8) ** -0.5, 0.375, ((0, 32),), jnp.float32),
        "ffn_gain": jnp.clip(1.0 + 0.15 * jax.random.normal(splits[11], (D,), jnp.float32), 0.25, 1.75),
        "w_gate": noise(splits[12], (D, FF), D ** -0.5, 0.125, ((0, 32),), jnp.float32),
        "w_up": noise(splits[13], (D, FF), D ** -0.5, 0.125, ((0, 32),), jnp.float32),
        "w_down": noise(splits[14], (FF, D), FF ** -0.5, 0.078125, ((0, 32),), jnp.float32),
    }


@jax.custom_vjp
def low(v):
    return lax.optimization_barrier(v.astype(jnp.bfloat16)).astype(jnp.float32)

@jax.custom_vjp
def low_back(v):
    return v

def low_keep(v):
    return (low(v), None)

def low_pass(kept, grad):
    return (grad,)

def back_keep(v):
    return (v, None)

def back_low(kept, grad):
    return (low(grad),)
low.defvjp(low_keep, low_pass)
low_back.defvjp(back_keep, back_low)

def product(left, right):
    return jnp.dot(left, right, precision=lax.Precision.HIGHEST)

def rms_norm(values, gain_vec):
    return values * lax.rsqrt(lax.optimization_barrier(jnp.mean(values * values, axis=-1, keepdims=True)) + 1e-06) * gain_vec

def short_conv(values, taps):
    total = values * taps[:, 0]
    for shift in range(1, CONV_K):
        moved = jnp.concatenate([jnp.zeros((shift, values.shape[1]), jnp.float32), values[:-shift]], axis=0)
        total = total + moved * taps[:, shift]
    return total

def taylor(values):
    count = values.shape[0]
    scaled = values.reshape(count, HEADS, FEAT).transpose(1, 0, 2) * FEAT ** (-0.25)
    outer = (scaled[:, :, :, None] * scaled[:, :, None, :]).reshape(HEADS, count, FEAT * FEAT) * 0.5 ** 0.5
    return jnp.concatenate([jnp.ones((HEADS, count, 1), jnp.float32), scaled, outer], axis=2)

def slot_forward(params, inputs, length):
    g_one, taps, wq, wk, wv, wq_win, wk_win, wo, g_two, wg, wu, wd = params
    count = inputs.shape[0]
    place = jnp.arange(count, dtype=jnp.int32)
    is_valid = (place < length).astype(jnp.float32)
    causal = place[:, None] >= place[None, :]
    in_window = causal & (place[:, None] - place[None, :] < WINDOW) & (place[None, :] < length)
    conv_low = low(low_back(short_conv(rms_norm(inputs, g_one), taps)))
    query = low_back(product(conv_low, wq))
    key_lin = low_back(product(conv_low, wk))
    value = low(low_back(product(conv_low, wv))).reshape(count, HEADS, VHEAD)
    query_win = low(low_back(product(conv_low, wq_win))).reshape(count, HEADS, VHEAD)
    key_win = low(low_back(product(conv_low, wk_win))).reshape(count, HEADS, VHEAD)
    feat_query = low(taylor(query))
    feat_key = low(taylor(key_lin) * is_valid[None, :, None])
    kernel = low_back(jnp.einsum('htf,hsf->hts', feat_query, feat_key, precision=lax.Precision.HIGHEST)) * causal.astype(jnp.float32)[None]
    share = low(kernel / lax.optimization_barrier(jnp.sum(kernel, axis=2, keepdims=True)))
    linear_out = jnp.einsum('hts,she->the', share, value, precision=lax.Precision.HIGHEST)
    raw_scores = low_back(jnp.einsum('the,she->hts', query_win, key_win, precision=lax.Precision.HIGHEST))
    logits = jnp.where(in_window[None], raw_scores * VHEAD ** (-0.5), -1e+30)
    probs = low(jax.nn.softmax(logits, axis=2))
    window_out = jnp.einsum('hts,she->the', probs, value, precision=lax.Precision.HIGHEST)
    mixed = low(low_back((linear_out + window_out).reshape(count, D)))
    resid = inputs + low_back(product(mixed, wo))
    normed = low(low_back(rms_norm(resid, g_two)))
    gate_pre = low_back(product(normed, wg))
    up_pre = low_back(product(normed, wu))
    hidden = low(low_back(jax.nn.silu(gate_pre) * up_pre))
    return (resid + low_back(product(hidden, wd))) * is_valid[:, None]

def reference(tokens, lengths, cotangent, norm_gain, conv_weight, w_query, w_key, w_value, w_query_window, w_key_window, w_out, ffn_gain, w_gate, w_up, w_down):
    masters = (norm_gain, conv_weight, w_query, w_key, w_value, w_query_window, w_key_window, w_out, ffn_gain, w_gate, w_up, w_down)
    inputs = tokens.astype(jnp.float32).reshape(DEVICES, TOK_DEV, D)

    def whole(slots, params):
        lowered = tuple((low(item) for item in params))

        def single(pair):
            return slot_forward(lowered, pair[0], pair[1])
        return lax.map(jax.checkpoint(single), (slots, lengths))
    result, pull = jax.vjp(whole, inputs, masters)
    grad_in, grads = pull(cotangent.astype(jnp.float32).reshape(DEVICES, TOK_DEV, D))
    return (result.reshape(TOKENS, D).astype(jnp.bfloat16), grad_in.reshape(TOKENS, D).astype(jnp.bfloat16), grads[0], grads[1], grads[2], grads[3], grads[4], grads[5], grads[6], grads[7], grads[8], grads[9], grads[10], grads[11])
```

```python
import functools

import jax
import jax.numpy as jnp
from jax import lax
from jax.experimental import pallas as pl
from jax.experimental.pallas import tpu as pltpu
from jax.sharding import PartitionSpec as P

D = 2048
HEADS = 16
FEAT = 16
WINDOW = 64
CONV_K = 3
VHEAD = 128
GROUP = 4
HEADS_G = HEADS // GROUP
LIN_G = HEADS_G * FEAT
WIN_G = HEADS_G * VHEAD
PACK = 2 * LIN_G + 3 * WIN_G

low = jnp.bfloat16
f32 = jnp.float32

CYCLES = {8: (0, 2, 4, 6, 7, 5, 3, 1)}


def dot(left, right, over_left, over_right):
    return lax.dot_general(
        left, right, (((over_left,), (over_right,)), ((), ())), preferred_element_type=f32
    )


def product(left, right):
    return dot(left, right, 1, 0)


def product_tn(left, right):
    return dot(left, right, 0, 0)


def product_nt(left, right):
    return dot(left, right, 1, 1)


def rms_norm(values, gain_vec):
    return values * lax.rsqrt(jnp.mean(values * values, axis=-1, keepdims=True) + 1e-06) * gain_vec


def short_conv(values, taps):
    total = values * taps[0]
    for shift in range(1, CONV_K):
        moved = jnp.concatenate(
            [jnp.zeros((shift, values.shape[1]), f32), values[:-shift]], axis=0
        )
        total = total + moved * taps[shift]
    return total


def front_part(inputs, g_one, taps):
    return short_conv(rms_norm(inputs, g_one), taps)


def head_parts(pack_ref, head, keep, in_window):
    query = pack_ref[:, FEAT * head : FEAT * (head + 1)].astype(low)
    key = pack_ref[:, LIN_G + FEAT * head : LIN_G + FEAT * (head + 1)].astype(low)
    start = 2 * LIN_G + VHEAD * head
    value = pack_ref[:, start : start + VHEAD].astype(low)
    start += WIN_G
    query_win = pack_ref[:, start : start + VHEAD].astype(low)
    start += WIN_G
    key_win = pack_ref[:, start : start + VHEAD].astype(low)
    scores = product_nt(query, key) * FEAT**-0.5
    kernel = jnp.where(keep, 1.0 + scores + 0.5 * scores * scores, 0.0)
    over = 1.0 / jnp.sum(kernel, axis=1, keepdims=True)
    share = kernel * over
    logits = jnp.where(in_window, product_nt(query_win, key_win) * VHEAD**-0.5, -1e30)
    raised = jnp.exp(logits - jnp.max(logits, axis=1, keepdims=True))
    probs = raised * (1.0 / jnp.sum(raised, axis=1, keepdims=True))
    return query, key, value, query_win, key_win, scores, over, share, probs


def masks(length, count):
    row = lax.broadcasted_iota(jnp.int32, (count, count), 0)
    col = lax.broadcasted_iota(jnp.int32, (count, count), 1)
    keep = (row >= col) & (col < length)
    return keep, keep & (row - col < WINDOW)


def mix_kernel(lens_ref, pack_ref, mixed_ref):
    keep, in_window = masks(lens_ref[pl.program_id(0)], pack_ref.shape[0])
    for head in range(HEADS_G):
        parts = head_parts(pack_ref, head, keep, in_window)
        value, share, probs = parts[2], parts[7], parts[8]
        out = product((share + probs).astype(low), value)
        mixed_ref[:, VHEAD * head : VHEAD * (head + 1)] = out.astype(low)


def mix_back_kernel(lens_ref, pack_ref, grad_ref, out_ref):
    keep, in_window = masks(lens_ref[pl.program_id(0)], pack_ref.shape[0])
    grad_query, grad_key = [], []
    for head in range(HEADS_G):
        query, key, value, query_win, key_win, scores, over, share, probs = head_parts(
            pack_ref, head, keep, in_window
        )
        grad = grad_ref[:, VHEAD * head : VHEAD * (head + 1)]
        weights = product_nt(grad, value)
        grad_raw = probs * (weights - jnp.sum(weights * probs, axis=1, keepdims=True))
        grad_raw = (grad_raw * VHEAD**-0.5).astype(low)
        centred = weights - jnp.sum(weights * share, axis=1, keepdims=True)
        grad_scores = jnp.where(keep, centred * (over * FEAT**-0.5) * (1.0 + scores), 0.0)
        grad_scores = grad_scores.astype(low)
        start = 2 * LIN_G + VHEAD * head
        out_ref[:, start : start + VHEAD] = product_tn((share + probs).astype(low), grad).astype(low)
        start += WIN_G
        out_ref[:, start : start + VHEAD] = product(grad_raw, key_win).astype(low)
        start += WIN_G
        out_ref[:, start : start + VHEAD] = product_tn(grad_raw, query_win).astype(low)
        grad_query.append(product(grad_scores, key).astype(low))
        grad_key.append(product_tn(grad_scores, query).astype(low))
    out_ref[:, : 2 * LIN_G] = jnp.concatenate(grad_query + grad_key, axis=1)


def per_sequence(body, name, count, widths, out_width, out_type, lens, *arrays):
    return pl.pallas_call(
        body,
        grid=(GROUP,),
        in_specs=[pl.BlockSpec(memory_space=pltpu.SMEM)]
        + [pl.BlockSpec((count, width), lambda i: (i, 0)) for width in widths],
        out_specs=pl.BlockSpec((count, out_width), lambda i: (i, 0)),
        out_shape=jax.ShapeDtypeStruct((GROUP * count, out_width), out_type),
        compiler_params=pltpu.CompilerParams(vmem_limit_bytes=32 * 1024 * 1024),
        cost_estimate=pl.CostEstimate(
            flops=2_000_000_000, bytes_accessed=10_000_000, transcendentals=1_000_000
        ),
        name=name,
    )(lens, *arrays)


def swap(value, over):
    return lax.ppermute(value, "grp", [(i, i ^ over) for i in range(GROUP)])


def group_gather(own):
    peer = swap(own, 1)
    across = swap(own, 2)
    return own, peer, across, swap(across, 1)


def group_sum(parts):
    across = (parts[2].astype(f32) + swap(parts[3], 1).astype(f32)).astype(low)
    return parts[0].astype(f32) + swap(parts[1], 1).astype(f32) + swap(across, 2).astype(f32)


def group_exchange(blocks, me):
    def pick(r):
        return lax.dynamic_index_in_dim(blocks, me ^ r, 0, keepdims=False)

    got = jnp.stack([pick(0)] + [swap(pick(r), r) for r in range(1, GROUP)])
    return [lax.dynamic_index_in_dim(got, me ^ j, 0, keepdims=False) for j in range(GROUP)]


def steps_of(axis, size):
    step = 1
    while step < size:
        yield axis, size, step
        step *= 2


def everywhere(value, wide_size):
    stack = value[None]
    for axis, size, step in list(steps_of("wide", wide_size)) + list(steps_of("grp", GROUP)):
        other = lax.ppermute(stack, axis, [(i, i ^ step) for i in range(size)])
        upper = (lax.axis_index(axis) & step) > 0
        stack = jnp.where(
            upper, jnp.concatenate([other, stack], 0), jnp.concatenate([stack, other], 0)
        )
    return stack


def sum_everywhere(value, wide_size):
    for axis, size, step in list(steps_of("grp", GROUP)) + list(steps_of("wide", wide_size)):
        value = value + lax.ppermute(value, axis, [(i, i ^ step) for i in range(size)])
    return value


def wide_gather(block, at, size):
    if size not in CYCLES:
        return jnp.moveaxis(lax.all_gather(block, "wide"), 0, at)
    cycle = CYCLES[size]
    order = jnp.array(cycle, jnp.int32)
    place = jnp.array([cycle.index(i) for i in range(size)], jnp.int32)[lax.axis_index("wide")]
    split = 0 if at == 1 else 2
    halves = jnp.split(block, 2, axis=split)
    whole = jnp.zeros(block.shape[:at] + (size,) + block.shape[at:], block.dtype)
    for step in range(size):
        for d in (0, 1):
            index = [jnp.int32(0)] * 4
            index[at] = order[(place - step if d == 0 else place + step) % size]
            index[split if at == 1 else 3] = jnp.int32(d * halves[0].shape[split])
            whole = lax.dynamic_update_slice(whole, jnp.expand_dims(halves[d], at), index)
            if step < size - 1:
                way = [(cycle[i], cycle[(i + 1) % size]) for i in range(size)]
                if d == 1:
                    way = [(to, of) for of, to in way]
                halves[d] = lax.ppermute(halves[d], "wide", way)
    return whole


def wide_sum(terms, at, size):
    split = 0 if at == 1 else 3
    if size not in CYCLES:
        full = lax.psum_scatter(terms.astype(f32), "wide", scatter_dimension=at, tiled=True)
        return jnp.split(jnp.squeeze(full, at), 2, axis=0 if at == 1 else 2)
    cycle = CYCLES[size]
    order = jnp.array(cycle, jnp.int32)
    place = jnp.array([cycle.index(i) for i in range(size)], jnp.int32)[lax.axis_index("wide")]
    extent = list(terms.shape)
    extent[at] = 1
    extent[split] //= 2
    sums = [None, None]
    for step in range(size):
        for d in (0, 1):
            index = [jnp.int32(0)] * 4
            index[at] = order[(place - step - 1 if d == 0 else place + step + 1) % size]
            index[split] = jnp.int32(d * extent[split])
            mine = jnp.squeeze(lax.dynamic_slice(terms, index, extent), at)
            if step == 0:
                sums[d] = mine
            else:
                sums[d] = sums[d].astype(f32) + mine.astype(f32)
            if step < size - 1:
                way = [(cycle[i], cycle[(i + 1) % size]) for i in range(size)]
                if d == 1:
                    way = [(to, of) for of, to in way]
                sums[d] = lax.ppermute(sums[d].astype(low), "wide", way)
    return sums


def shards(
    tokens,
    lengths,
    cotangent,
    norm_gain,
    conv_weight,
    w_query,
    w_key,
    w_value,
    w_query_window,
    w_key_window,
    w_out,
    ffn_gain,
    w_gate,
    w_up,
    w_down,
    *,
    wide_size,
):
    me = lax.axis_index("grp")
    spot = me * wide_size + lax.axis_index("wide")
    count = tokens.shape[0]
    rows = w_query.shape[0]
    hid_rows = w_down.shape[0]
    hid_g = w_gate.shape[1] // GROUP
    length = lengths[0]
    is_valid = (jnp.arange(count, dtype=jnp.int32) < length).astype(f32)

    def by_columns(weight):
        width = weight.shape[1] // GROUP
        return weight.astype(low).reshape(rows, GROUP, width).transpose(1, 0, 2)

    mixer_blocks = jnp.concatenate(
        [by_columns(x) for x in (w_query, w_key, w_value, w_query_window, w_key_window)], axis=2
    )
    mixer_shard = jnp.stack(group_exchange(mixer_blocks, me))
    w_mix = wide_gather(mixer_shard, 1, wide_size).reshape(D, PACK)
    wo = wide_gather(w_out.astype(low)[None].reshape(rows, 1, D), 0, wide_size).reshape(WIN_G, D)
    gate_shard = jnp.stack(group_exchange(by_columns(w_gate), me))
    up_shard = jnp.stack(group_exchange(by_columns(w_up), me))
    wg = wide_gather(gate_shard, 1, wide_size).reshape(D, hid_g)
    wu = wide_gather(up_shard, 1, wide_size).reshape(D, hid_g)
    wd = wide_gather(w_down.astype(low).reshape(hid_rows, 1, D), 0, wide_size).reshape(hid_g, D)

    small = jnp.concatenate(
        [
            norm_gain[None],
            conv_weight.T,
            ffn_gain[None],
            jnp.broadcast_to(length.astype(f32), (1, rows)),
            jnp.zeros((2, rows), f32),
        ],
        axis=0,
    ).astype(low)
    small_all = everywhere(small, wide_size)
    g_one, tap_0, tap_1, tap_2, g_two = [
        small_all[:, i].reshape(D).astype(f32) for i in range(5)
    ]
    taps = jnp.stack([tap_0, tap_1, tap_2])
    group_lens = small_all[:, 5, 0].reshape(GROUP, wide_size)
    group_lens = lax.dynamic_index_in_dim(group_lens, lax.axis_index("wide"), 1, keepdims=False)
    group_lens = group_lens.astype(jnp.int32)[me ^ jnp.arange(GROUP, dtype=jnp.int32)]

    inputs = tokens.astype(f32)
    conv_out, front_pull = jax.vjp(front_part, inputs, g_one, taps)
    conv_low = jnp.concatenate(group_gather(conv_out.astype(low)), axis=0)
    grad_outer = cotangent.astype(f32) * is_valid[:, None]
    down_in = jnp.concatenate(group_gather(grad_outer.astype(low)), axis=0)

    pack = product(conv_low, w_mix)
    mixed = per_sequence(
        mix_kernel, "mix", count, (PACK,), WIN_G, low, group_lens, pack
    )

    def partial_sum(make):
        far = make(slice(2 * count, 4 * count)).astype(low)
        near = make(slice(0, 2 * count)).astype(low)
        return group_sum([near[:count], near[count:], far[:count], far[count:]])

    resid = inputs + partial_sum(lambda part: product(mixed[part], wo))
    normed_f, middle_pull = jax.vjp(rms_norm, resid, g_two)
    normed = jnp.concatenate(group_gather(normed_f.astype(low)), axis=0)
    gate_pre = product(normed, wg)
    up_pre = product(normed, wu)
    sigma = jax.nn.sigmoid(gate_pre)
    silu_gate = gate_pre * sigma
    hidden = (silu_gate * up_pre).astype(low)
    down = partial_sum(lambda part: product(hidden[part], wd))
    block_out = ((resid + down) * is_valid[:, None]).astype(low)

    grad_down = product_tn(hidden, down_in).astype(low)
    grad_hidden = product_nt(down_in, wd).astype(low).astype(f32)
    grad_gate_pre = (grad_hidden * up_pre * sigma * (1.0 + gate_pre * (1.0 - sigma))).astype(low)
    grad_up_pre = (grad_hidden * silu_gate).astype(low)
    grad_normed = partial_sum(
        lambda part: product_nt(grad_gate_pre[part], wg) + product_nt(grad_up_pre[part], wu)
    )
    grad_gate = product_tn(normed, grad_gate_pre).astype(low)
    grad_up = product_tn(normed, grad_up_pre).astype(low)
    grad_resid_norm, grad_ffn_gain = middle_pull(grad_normed.astype(low).astype(f32))
    grad_resid = grad_outer + grad_resid_norm
    branch_in = jnp.concatenate(group_gather(grad_resid.astype(low)), axis=0)

    down_sums = wide_sum(grad_down.reshape(wide_size, hid_rows, 1, D), 0, wide_size)
    gate_sums = wide_sum(grad_gate.reshape(GROUP, wide_size, rows, hid_g), 1, wide_size)
    up_sums = wide_sum(grad_up.reshape(GROUP, wide_size, rows, hid_g), 1, wide_size)

    grad_mixed = product_nt(branch_in, wo).astype(low)
    grad_out = product_tn(mixed, branch_in).astype(low)
    grad_pack = per_sequence(
        mix_back_kernel, "mix_back", count, (PACK, WIN_G), PACK, low, group_lens, pack, grad_mixed
    )
    grad_mix = product_tn(conv_low, grad_pack).astype(low)
    grad_conv_low = partial_sum(lambda part: product_nt(grad_pack[part], w_mix))
    grad_front, grad_norm_gain, grad_taps = front_pull(grad_conv_low.astype(low).astype(f32))
    grad_tokens = (grad_resid + grad_front).astype(low)

    out_sums = wide_sum(grad_out.reshape(wide_size, rows, 1, D), 0, wide_size)
    mix_sums = wide_sum(grad_mix.reshape(GROUP, wide_size, rows, PACK), 1, wide_size)

    def to_owner(halves):
        return group_exchange(jnp.concatenate(halves, axis=0).astype(low), me)

    def widen(pieces):
        return jnp.concatenate([piece.astype(f32) for piece in pieces], axis=1)

    mix_pieces = to_owner(mix_sums)
    edges = [0, LIN_G, 2 * LIN_G, 2 * LIN_G + WIN_G, 2 * LIN_G + 2 * WIN_G, PACK]
    grad_query, grad_key, grad_value, grad_query_window, grad_key_window = [
        widen([piece[:, a:b] for piece in mix_pieces]) for a, b in zip(edges, edges[1:])
    ]
    gains = jnp.concatenate(
        [grad_norm_gain[None], grad_taps, grad_ffn_gain[None], jnp.zeros((3, D), f32)], axis=0
    )
    gains = sum_everywhere(gains, wide_size).reshape(8, GROUP * wide_size, rows)
    gains = lax.dynamic_index_in_dim(gains, spot, 1, keepdims=False)
    return (
        block_out,
        grad_tokens,
        gains[0],
        gains[1 : 1 + CONV_K].T,
        grad_query,
        grad_key,
        grad_value,
        grad_query_window,
        grad_key_window,
        jnp.concatenate(out_sums, axis=2).reshape(rows, D),
        gains[1 + CONV_K],
        widen(to_owner(gate_sums)),
        widen(to_owner(up_sums)),
        jnp.concatenate(down_sums, axis=2).reshape(hid_rows, D),
    )


def solution(mesh):
    rows = P(("grp", "wide"), None)
    flat = P(("grp", "wide"))
    return jax.shard_map(
        functools.partial(shards, wide_size=mesh.shape["wide"]),
        mesh=mesh,
        in_specs=(rows, flat, rows, flat, rows, rows, rows, rows, rows, rows, rows, flat, rows, rows, rows),
        out_specs=(rows, rows, flat, rows, rows, rows, rows, rows, rows, rows, flat, rows, rows, rows),
        check_vma=False,
    )
```

```python
import functools

import jax
import jax.numpy as jnp
from jax import lax
from jax.experimental import pallas as pl
from jax.experimental.pallas import tpu as pltpu
from jax.sharding import PartitionSpec as P

D = 2048
HEADS = 16
FEAT = 16
WINDOW = 64
CONV_K = 3
VHEAD = 128
GROUP = 4
HEADS_G = HEADS // GROUP
LIN_G = HEADS_G * FEAT
WIN_G = HEADS_G * VHEAD
PACK = 2 * LIN_G + 3 * WIN_G

low = jnp.bfloat16
f32 = jnp.float32

CYCLES = {8: (0, 2, 4, 6, 7, 5, 3, 1)}


def dot(left, right, over_left, over_right):
    return lax.dot_general(
        left, right, (((over_left,), (over_right,)), ((), ())), preferred_element_type=f32
    )


def product(left, right):
    return dot(left, right, 1, 0)


def product_tn(left, right):
    return dot(left, right, 0, 0)


def product_nt(left, right):
    return dot(left, right, 1, 1)


def rms_norm(values, gain_vec):
    return values * lax.rsqrt(jnp.mean(values * values, axis=-1, keepdims=True) + 1e-06) * gain_vec


def short_conv(values, taps):
    total = values * taps[0]
    for shift in range(1, CONV_K):
        moved = jnp.concatenate(
            [jnp.zeros((shift, values.shape[1]), f32), values[:-shift]], axis=0
        )
        total = total + moved * taps[shift]
    return total


def front_part(inputs, g_one, taps):
    return short_conv(rms_norm(inputs, g_one), taps)


def head_parts(pack_ref, head, keep, in_window):
    query = pack_ref[:, FEAT * head : FEAT * (head + 1)].astype(low)
    key = pack_ref[:, LIN_G + FEAT * head : LIN_G + FEAT * (head + 1)].astype(low)
    start = 2 * LIN_G + VHEAD * head
    value = pack_ref[:, start : start + VHEAD].astype(low)
    start += WIN_G
    query_win = pack_ref[:, start : start + VHEAD].astype(low)
    start += WIN_G
    key_win = pack_ref[:, start : start + VHEAD].astype(low)
    scores = product_nt(query, key) * FEAT**-0.5
    kernel = jnp.where(keep, 1.0 + scores + 0.5 * scores * scores, 0.0)
    over = 1.0 / jnp.sum(kernel, axis=1, keepdims=True)
    share = kernel * over
    logits = jnp.where(in_window, product_nt(query_win, key_win) * VHEAD**-0.5, -1e30)
    raised = jnp.exp(logits - jnp.max(logits, axis=1, keepdims=True))
    probs = raised * (1.0 / jnp.sum(raised, axis=1, keepdims=True))
    return query, key, value, query_win, key_win, scores, over, share, probs


def masks(length, count):
    row = lax.broadcasted_iota(jnp.int32, (count, count), 0)
    col = lax.broadcasted_iota(jnp.int32, (count, count), 1)
    keep = (row >= col) & (col < length)
    return keep, keep & (row - col < WINDOW)


def mix_kernel(lens_ref, pack_ref, mixed_ref):
    keep, in_window = masks(lens_ref[pl.program_id(0)], pack_ref.shape[0])
    for head in range(HEADS_G):
        parts = head_parts(pack_ref, head, keep, in_window)
        value, share, probs = parts[2], parts[7], parts[8]
        out = product((share + probs).astype(low), value)
        mixed_ref[:, VHEAD * head : VHEAD * (head + 1)] = out.astype(low)


def mix_back_kernel(lens_ref, pack_ref, grad_ref, out_ref):
    keep, in_window = masks(lens_ref[pl.program_id(0)], pack_ref.shape[0])
    grad_query, grad_key = [], []
    for head in range(HEADS_G):
        query, key, value, query_win, key_win, scores, over, share, probs = head_parts(
            pack_ref, head, keep, in_window
        )
        grad = grad_ref[:, VHEAD * head : VHEAD * (head + 1)]
        weights = product_nt(grad, value)
        grad_raw = probs * (weights - jnp.sum(weights * probs, axis=1, keepdims=True))
        grad_raw = (grad_raw * VHEAD**-0.5).astype(low)
        centred = weights - jnp.sum(weights * share, axis=1, keepdims=True)
        grad_scores = jnp.where(keep, centred * (over * FEAT**-0.5) * (1.0 + scores), 0.0)
        grad_scores = grad_scores.astype(low)
        start = 2 * LIN_G + VHEAD * head
        out_ref[:, start : start + VHEAD] = product_tn((share + probs).astype(low), grad).astype(low)
        start += WIN_G
        out_ref[:, start : start + VHEAD] = product(grad_raw, key_win).astype(low)
        start += WIN_G
        out_ref[:, start : start + VHEAD] = product_tn(grad_raw, query_win).astype(low)
        grad_query.append(product(grad_scores, key).astype(low))
        grad_key.append(product_tn(grad_scores, query).astype(low))
    out_ref[:, : 2 * LIN_G] = jnp.concatenate(grad_query + grad_key, axis=1)


def per_sequence(body, name, count, widths, out_width, out_type, lens, *arrays):
    return pl.pallas_call(
        body,
        grid=(GROUP,),
        in_specs=[pl.BlockSpec(memory_space=pltpu.SMEM)]
        + [pl.BlockSpec((count, width), lambda i: (i, 0)) for width in widths],
        out_specs=pl.BlockSpec((count, out_width), lambda i: (i, 0)),
        out_shape=jax.ShapeDtypeStruct((GROUP * count, out_width), out_type),
        compiler_params=pltpu.CompilerParams(vmem_limit_bytes=32 * 1024 * 1024),
        cost_estimate=pl.CostEstimate(
            flops=2_000_000_000, bytes_accessed=10_000_000, transcendentals=1_000_000
        ),
        name=name,
    )(lens, *arrays)


bar = lax.optimization_barrier


def swap(value, over):
    return lax.ppermute(value, "grp", [(i, i ^ over) for i in range(GROUP)])


def group_gather(own):
    peer = swap(own, 1)
    across = swap(own, 2)
    return own, peer, across, swap(across, 1)


def reorder(stack):
    me = lax.axis_index("grp")
    return jnp.concatenate([lax.dynamic_slice_in_dim(stack, me ^ r, 1) for r in range(GROUP)])


def after(token, *values):
    return bar((*values, token))[:-1]


def steps_of(axis, size):
    step = 1
    while step < size:
        yield axis, size, step
        step *= 2


def everywhere(value, wide_size):
    stack = value[None]
    for axis, size, step in list(steps_of("wide", wide_size)) + list(steps_of("grp", GROUP)):
        other = lax.ppermute(stack, axis, [(i, i ^ step) for i in range(size)])
        upper = (lax.axis_index(axis) & step) > 0
        stack = jnp.where(
            upper, jnp.concatenate([other, stack], 0), jnp.concatenate([stack, other], 0)
        )
    return stack


def sum_everywhere(value, wide_size):
    for axis, size, step in list(steps_of("grp", GROUP)) + list(steps_of("wide", wide_size)):
        value = value + lax.ppermute(value, axis, [(i, i ^ step) for i in range(size)])
    return value


SMEM = pl.BlockSpec(memory_space=pltpu.SMEM)
VMEM = pl.BlockSpec(memory_space=pltpu.VMEM)
ANY = pl.BlockSpec(memory_space=pl.ANY)


def params(mib):
    return pltpu.CompilerParams(vmem_limit_bytes=mib * 1024 * 1024)


def cost(nbytes, flops=0):
    return pl.CostEstimate(flops=flops, bytes_accessed=nbytes, transcendentals=0)


def split_mixer(table, weights):
    rows = weights[0].shape[0]

    def body(table_ref, *refs):
        out = refs[-1]
        for j in range(GROUP):
            pieces = []
            for ref in refs[:-1]:
                width = ref.shape[1] // GROUP
                pieces.append(ref[:, j * width : (j + 1) * width].astype(low))
            out[j ^ table_ref[0]] = jnp.concatenate(pieces, axis=1)

    return pl.pallas_call(
        body,
        in_specs=[SMEM] + [VMEM] * len(weights),
        out_specs=VMEM,
        out_shape=jax.ShapeDtypeStruct((GROUP, rows, PACK), low),
        compiler_params=params(24),
        cost_estimate=cost(rows * PACK * GROUP * 6),
        name="split_mixer",
    )(table, *weights)


def split_gate_up(table, w_gate, w_up, wide_size, part, part_p):
    rows = w_gate.shape[0]
    hid_p = wide_size * part_p

    def body(table_ref, gate_ref, up_ref, out):
        fill = jnp.zeros((rows, part_p - part), f32)
        for j in range(GROUP):
            pieces = []
            for ref in (gate_ref, up_ref):
                for w in range(wide_size):
                    start = (j * wide_size + w) * part
                    pieces += [ref[:, start : start + part], fill]
            out[j ^ table_ref[0]] = jnp.concatenate(pieces, axis=1).astype(low)

    return pl.pallas_call(
        body,
        in_specs=[SMEM, VMEM, VMEM],
        out_specs=VMEM,
        out_shape=jax.ShapeDtypeStruct((GROUP, rows, 2 * hid_p), low),
        compiler_params=params(24),
        cost_estimate=cost(rows * hid_p * GROUP * 12),
        name="split_gate_up",
    )(table, w_gate, w_up)


def merge_gate_up(table, pieces, wide_size, part, part_p):
    rows = pieces[0].shape[0]
    hid_p = wide_size * part_p
    full = jax.ShapeDtypeStruct((rows, GROUP * wide_size * part), f32)

    def body(table_ref, a, b, c, d, gate_ref, up_ref, held):
        for r, ref in enumerate((a, b, c, d)):
            held[r] = ref[...].astype(f32)
        for at, out in ((0, gate_ref), (hid_p, up_ref)):
            for j in range(GROUP):
                block = held[j ^ table_ref[0]]
                parts = [block[:, at + w * part_p : at + w * part_p + part] for w in range(wide_size)]
                start = j * wide_size * part
                out[:, start : start + wide_size * part] = jnp.concatenate(parts, axis=1)

    return pl.pallas_call(
        body,
        in_specs=[SMEM] + [VMEM] * 4,
        out_specs=[VMEM, VMEM],
        out_shape=[full, full],
        scratch_shapes=[pltpu.VMEM((GROUP, rows, 2 * hid_p), f32)],
        compiler_params=params(24),
        cost_estimate=cost(rows * hid_p * GROUP * 12),
        name="merge_gate_up",
    )(table, *pieces)


def merge_mixer(table, pieces):
    rows = pieces[0].shape[0]
    widths = [LIN_G, LIN_G, WIN_G, WIN_G, WIN_G]

    def body(table_ref, a, b, c, d, *refs):
        outs, held = refs[:-1], refs[-1]
        for r, ref in enumerate((a, b, c, d)):
            held[r] = ref[...].astype(f32)
        blocks = [held[j ^ table_ref[0]] for j in range(GROUP)]
        at = 0
        for width, out in zip(widths, outs):
            out[...] = jnp.concatenate([block[:, at : at + width] for block in blocks], axis=1)
            at += width

    return pl.pallas_call(
        body,
        in_specs=[SMEM] + [VMEM] * 4,
        out_specs=[VMEM] * 5,
        out_shape=[jax.ShapeDtypeStruct((rows, GROUP * width), f32) for width in widths],
        scratch_shapes=[pltpu.VMEM((GROUP, rows, PACK), f32)],
        compiler_params=params(24),
        cost_estimate=cost(rows * PACK * GROUP * 6),
        name="merge_mixer",
    )(table, *pieces)


def place(table, ways, grouped, size):
    piece = ways[0][0]
    rows, width = piece.shape[-2:]
    shape = (GROUP, size, rows, width) if grouped else (size, rows, 2 * width)

    def body(table_ref, *refs):
        out, sems = refs[-2:]
        copies = []
        for d in (0, 1):
            for s in range(size):
                ref = refs[d * size + s]
                owner = table_ref[1 + d * size + s]
                if grouped:
                    for i in range(2):
                        copies.append((ref.at[i], out.at[(2 * d + i) ^ table_ref[0], owner]))
                else:
                    copies.append((ref, out.at[owner, :, d * width : (d + 1) * width]))
        copies = [pltpu.make_async_copy(of, to, sems.at[k]) for k, (of, to) in enumerate(copies)]
        for copy in copies:
            copy.start()
        for copy in copies:
            copy.wait()

    return pl.pallas_call(
        body,
        in_specs=[SMEM] + [ANY] * (2 * size),
        out_specs=ANY,
        out_shape=jax.ShapeDtypeStruct(shape, low),
        scratch_shapes=[pltpu.SemaphoreType.DMA(((4 if grouped else 2) * size,))],
        compiler_params=params(2),
        cost_estimate=cost(8 * size * rows * width * piece.ndim),
        name="place",
    )(table, *ways[0], *ways[1])


def pick_add(table, terms, got, step, size, keep_rows=None):
    grouped = terms.ndim == 4
    rows, width = terms.shape[-2:]
    k = (step + 1) % size
    if not grouped:
        width //= 2

    def body(table_ref, *refs):
        mine, outs = refs[:2], refs[-2:] if keep_rows is None else refs[-1:]
        for d in (0, 1):
            total = mine[d][...].reshape(rows, width).astype(f32)
            if got is not None:
                total = total + refs[2 + d][...].reshape(rows, width).astype(f32)
            if keep_rows is None:
                outs[d][...] = total.reshape(outs[d].shape).astype(low)
            else:
                outs[0][:, d * width : (d + 1) * width] = total[:keep_rows]

    def owner(table_ref, d):
        return table_ref[1 + d * size + k]

    if grouped:
        grid = (2,)
        term_specs = [
            pl.BlockSpec(
                (1, 1, rows, width),
                lambda i, t, d=d: ((2 * d + i) ^ t[0], owner(t, d), 0, 0),
            )
            for d in (0, 1)
        ]
        piece = pl.BlockSpec((1, rows, width), lambda i, t: (i, 0, 0))
        shape = jax.ShapeDtypeStruct((2, rows, width), low)
    else:
        grid = (1,)
        term_specs = [
            pl.BlockSpec((1, rows, width), lambda i, t, d=d: (owner(t, d), 0, d)) for d in (0, 1)
        ]
        piece = pl.BlockSpec((rows, width), lambda i, t: (0, 0))
        shape = jax.ShapeDtypeStruct((rows, width), low)
    out_specs, out_shape = [piece, piece], [shape, shape]
    if keep_rows is not None:
        out_specs = [pl.BlockSpec((keep_rows, 2 * width), lambda i, t: (0, 0))]
        out_shape = [jax.ShapeDtypeStruct((keep_rows, 2 * width), f32)]
    came = [] if got is None else list(got)

    return pl.pallas_call(
        body,
        grid_spec=pltpu.PrefetchScalarGridSpec(
            num_scalar_prefetch=1,
            grid=grid,
            in_specs=term_specs + [piece] * len(came),
            out_specs=out_specs,
        ),
        out_shape=out_shape,
        compiler_params=params(16),
        cost_estimate=cost(8 * rows * width * 3),
        name="pick_add",
    )(table, terms, terms, *came)


def round_ring(cycle, d):
    size = len(cycle)
    way = [(cycle[i], cycle[(i + 1) % size]) for i in range(size)]
    return way if d == 0 else [(to, of) for of, to in way]


class GatherRing:
    def __init__(self, halves, grouped, size, table):
        self.held = [[half] for half in halves]
        self.grouped, self.size, self.table = grouped, size, table
        self.steps = size - 1 if size in CYCLES else 0

    def step(self, token=None):
        if self.steps == 0:
            return
        self.steps -= 1
        for d, held in enumerate(self.held):
            value = held[-1] if token is None else after(token, held[-1])[0]
            held.append(lax.ppermute(value, "wide", round_ring(CYCLES[self.size], d)))

    def done(self, token=None):
        while self.steps:
            self.step()
        if self.size in CYCLES:
            ways = self.held
            if token is not None:
                ways = [list(after(token, *held)) for held in ways]
            out = place(self.table, ways, self.grouped, self.size)
        elif self.grouped:
            block = jnp.concatenate([self.held[0][0], self.held[1][0]], axis=0)
            out = jnp.moveaxis(lax.all_gather(block, "wide"), 0, 1)
            out = reorder(out)
        else:
            block = jnp.concatenate([self.held[0][0], self.held[1][0]], axis=1)
            out = lax.all_gather(block, "wide")
        return out.reshape(-1, out.shape[-1])


class SumRing:
    def __init__(self, terms, size, table, keep_rows=None):
        self.terms, self.size, self.table, self.keep_rows = terms, size, table, keep_rows
        self.at, self.got = 0, None
        self.left = size - 1 if size in CYCLES else 0

    def step(self, token=None):
        if self.left == 0:
            return
        self.left -= 1
        got = self.got
        if token is not None:
            got = after(token, *got) if got is not None else None
            if got is None:
                self.terms = after(token, self.terms)[0]
        sums = pick_add(self.table, self.terms, got, self.at, self.size)
        self.at += 1
        cycle = CYCLES[self.size]
        self.got = [lax.ppermute(sums[d], "wide", round_ring(cycle, d)) for d in (0, 1)]

    def done(self):
        while self.left:
            self.step()
        if self.size in CYCLES:
            out = pick_add(
                self.table, self.terms, self.got, self.at, self.size, self.keep_rows
            )
            return out if self.keep_rows is None else out[0]
        if self.keep_rows is None:
            full = lax.psum_scatter(
                self.terms.astype(f32), "wide", scatter_dimension=1, tiled=True
            )[:, 0]
            full = reorder(full).astype(low)
            return full[:2], full[2:]
        full = lax.psum_scatter(self.terms.astype(f32), "wide", scatter_dimension=0, tiled=True)
        return full[0, : self.keep_rows]


def table_of(wide_size):
    me = lax.axis_index("grp").astype(jnp.int32)
    if wide_size not in CYCLES:
        return me[None]
    cycle = CYCLES[wide_size]
    rows = []
    for w in range(wide_size):
        at = cycle.index(w)
        rows.append(
            [cycle[(at - s) % wide_size] for s in range(wide_size)]
            + [cycle[(at + s) % wide_size] for s in range(wide_size)]
        )
    row = lax.dynamic_index_in_dim(
        jnp.array(rows, jnp.int32), lax.axis_index("wide"), 0, keepdims=False
    )
    return jnp.concatenate([me[None], row])


def shards(
    tokens,
    lengths,
    cotangent,
    norm_gain,
    conv_weight,
    w_query,
    w_key,
    w_value,
    w_query_window,
    w_key_window,
    w_out,
    ffn_gain,
    w_gate,
    w_up,
    w_down,
    *,
    wide_size,
):
    me = lax.axis_index("grp")
    spot = me * wide_size + lax.axis_index("wide")
    count = tokens.shape[0]
    rows = w_query.shape[0]
    part = w_down.shape[0]
    part_p = -(-part // 16) * 16
    hid_p = wide_size * part_p
    length = lengths[0]
    is_valid = (jnp.arange(count, dtype=jnp.int32) < length).astype(f32)
    table = table_of(wide_size)

    small = jnp.concatenate(
        [
            norm_gain[None],
            conv_weight.T,
            ffn_gain[None],
            jnp.broadcast_to(length.astype(f32), (1, rows)),
            jnp.zeros((2, rows), f32),
        ],
        axis=0,
    ).astype(low)
    small_all = everywhere(small, wide_size)

    half = D // 2
    out_low = w_out.astype(low)
    out_ring = GatherRing([out_low[:, :half], out_low[:, half:]], False, wide_size, table)
    mixer_blocks = split_mixer(table, (w_query, w_key, w_value, w_query_window, w_key_window))
    mixer_got = [mixer_blocks[0]] + [swap(mixer_blocks[r], r) for r in range(1, GROUP)]
    mix_ring = GatherRing(
        [jnp.stack(mixer_got[:2]), jnp.stack(mixer_got[2:])], True, wide_size, table
    )
    gu_blocks = split_gate_up(table, w_gate, w_up, wide_size, part, part_p)
    gu_blocks = after(mixer_got[3], gu_blocks)[0]
    gu_got = [gu_blocks[0]] + [swap(gu_blocks[r], r) for r in range(1, GROUP)]
    gu_ring = GatherRing([jnp.stack(gu_got[:2]), jnp.stack(gu_got[2:])], True, wide_size, table)
    down_low = jnp.pad(w_down.astype(low), ((0, part_p - part), (0, 0)))
    down_ring = GatherRing([down_low[:, :half], down_low[:, half:]], False, wide_size, table)

    g_one, tap_0, tap_1, tap_2, g_two = [
        small_all[:, i].reshape(D).astype(f32) for i in range(5)
    ]
    taps = jnp.stack([tap_0, tap_1, tap_2])
    group_lens = small_all[:, 5, 0].astype(jnp.int32).reshape(GROUP, wide_size)
    group_lens = lax.dynamic_index_in_dim(group_lens, lax.axis_index("wide"), 1, keepdims=False)
    group_lens = reorder(group_lens)

    inputs = tokens.astype(f32)
    conv_out, front_pull = jax.vjp(front_part, inputs, g_one, taps)
    conv_low = jnp.concatenate(group_gather(conv_out.astype(low)), axis=0)
    grad_outer = cotangent.astype(f32) * is_valid[:, None]
    down_own = after(conv_low, grad_outer.astype(low))[0]
    down_in = jnp.concatenate(group_gather(down_own), axis=0)

    for _ in range(3):
        out_ring.step()
    for _ in range(4):
        mix_ring.step()
        out_ring.step()
    token = mix_ring.held[0][-1]
    gu_ring.step(token)
    mix_ring.step()
    down_ring.step(token)
    mix_ring.step()
    mix_ring.step()
    w_mix = mix_ring.done()
    wo = out_ring.done()

    def advance(rings, token):
        for ring in rings:
            ring.step(token)

    ffn_rings = (gu_ring, down_ring)
    pack = product(conv_low, w_mix)
    advance(ffn_rings, pack)
    mixed = per_sequence(
        mix_kernel, "mix", count, (PACK,), WIN_G, low, group_lens, pack
    )
    advance(ffn_rings, mixed)

    def partial_sum(make, rings):
        far = make(slice(2 * count, 4 * count)).astype(low)
        over = swap(far[count:], 1)
        near = make(slice(0, 2 * count)).astype(low)
        peer = swap(near[count:], 1)
        across = (far[:count].astype(f32) + over.astype(f32)).astype(low)
        got = swap(across, 2)
        advance(rings, across)
        return near[:count].astype(f32) + peer.astype(f32) + got.astype(f32)

    resid = inputs + partial_sum(lambda part_: product(mixed[part_], wo), ffn_rings)
    normed_f, middle_pull = jax.vjp(rms_norm, resid, g_two)
    normed_own = normed_f.astype(low)
    advance(ffn_rings, normed_own)
    normed = jnp.concatenate(group_gather(normed_own), axis=0)
    advance(ffn_rings, normed)
    w_gu = gu_ring.done()
    gate_up = product(normed, w_gu)
    wd = down_ring.done()
    gate_pre, up_pre = gate_up[:, :hid_p], gate_up[:, hid_p:]
    sigma = jax.nn.sigmoid(gate_pre)
    silu_gate = gate_pre * sigma
    hidden = (silu_gate * up_pre).astype(low)

    grad_down = product_tn(hidden, down_in).astype(low)
    down_sum = SumRing(grad_down.reshape(wide_size, part_p, D), wide_size, table, part)
    down_sum.step()
    grad_hidden = product_nt(down_in, wd).astype(low).astype(f32)
    grad_gu = jnp.concatenate(
        [
            (grad_hidden * up_pre * sigma * (1.0 + gate_pre * (1.0 - sigma))).astype(low),
            (grad_hidden * silu_gate).astype(low),
        ],
        axis=1,
    )
    down_sum.step(grad_gu)
    grad_normed = partial_sum(lambda part_: product_nt(grad_gu[part_], w_gu), (down_sum,))
    grad_w_gu = product_tn(normed, grad_gu).astype(low)
    down_sum.step(grad_w_gu)
    gu_sum = SumRing(grad_w_gu.reshape(GROUP, wide_size, rows, 2 * hid_p), wide_size, table)
    gu_sum.step()
    grad_resid_norm, grad_ffn_gain = middle_pull(grad_normed.astype(low).astype(f32))
    grad_resid = grad_outer + grad_resid_norm
    branch_own = grad_resid.astype(low)
    ffn_sums = (down_sum, gu_sum)
    advance(ffn_sums, branch_own)
    branch_in = jnp.concatenate(group_gather(branch_own), axis=0)
    advance(ffn_sums, branch_in)
    grad_mixed = product_nt(branch_in, wo).astype(low)
    grad_pack = per_sequence(
        mix_back_kernel, "mix_back", count, (PACK, WIN_G), PACK, low, group_lens, pack, grad_mixed
    )
    advance(ffn_sums, grad_pack)
    grad_mix = product_tn(conv_low, grad_pack).astype(low)
    advance(ffn_sums, grad_mix)
    grad_conv_low = partial_sum(lambda part_: product_nt(grad_pack[part_], w_mix), ffn_sums)
    grad_out = product_tn(mixed, branch_in).astype(low)
    advance(ffn_sums, grad_out)
    grad_front, grad_norm_gain, grad_taps = front_pull(grad_conv_low.astype(low).astype(f32))
    grad_tokens = (grad_resid + grad_front).astype(low)
    advance(ffn_sums, grad_tokens)
    grad_w_down = down_sum.done()
    gu_halves = gu_sum.done()

    mix_sum = SumRing(grad_mix.reshape(GROUP, wide_size, rows, PACK), wide_size, table)
    out_sum = SumRing(grad_out.reshape(wide_size, rows, D), wide_size, table, rows)

    down = partial_sum(lambda part_: product(hidden[part_], wd), ())
    block_out = ((resid + down) * is_valid[:, None]).astype(low)

    def to_owner(halves):
        blocks = [halves[0][0], halves[0][1], halves[1][0], halves[1][1]]
        return [blocks[0]] + [swap(blocks[r], r) for r in range(1, GROUP)]

    grad_gate, grad_up = merge_gate_up(table, to_owner(gu_halves), wide_size, part, part_p)
    grad_w_out = out_sum.done()
    mixer_grads = merge_mixer(table, to_owner(mix_sum.done()))
    gains = jnp.concatenate(
        [grad_norm_gain[None], grad_taps, grad_ffn_gain[None], jnp.zeros((3, D), f32)], axis=0
    )
    gains = sum_everywhere(gains, wide_size).reshape(8, GROUP * wide_size, rows)
    gains = lax.dynamic_index_in_dim(gains, spot, 1, keepdims=False)
    return (
        block_out,
        grad_tokens,
        gains[0],
        gains[1 : 1 + CONV_K].T,
        *mixer_grads,
        grad_w_out,
        gains[1 + CONV_K],
        grad_gate,
        grad_up,
        grad_w_down,
    )


def solution(mesh):
    rows = P(("grp", "wide"), None)
    flat = P(("grp", "wide"))
    return jax.shard_map(
        functools.partial(shards, wide_size=mesh.shape["wide"]),
        mesh=mesh,
        in_specs=(rows, flat, rows, flat, rows, rows, rows, rows, rows, rows, rows, flat, rows, rows, rows),
        out_specs=(rows, rows, flat, rows, rows, rows, rows, rows, rows, rows, flat, rows, rows, rows),
        check_vma=False,
    )
```

```python
import functools

import jax
import jax.numpy as jnp
from jax import lax
from jax.experimental import pallas as pl
from jax.experimental.pallas import tpu as pltpu
from jax.sharding import PartitionSpec as P

D = 2048
HEADS = 16
FEAT = 16
WINDOW = 64
CONV_K = 3
VHEAD = 128
GROUP = 4
HEADS_G = HEADS // GROUP
LIN_G = HEADS_G * FEAT
WIN_G = HEADS_G * VHEAD
PACK = 2 * LIN_G + 3 * WIN_G

low = jnp.bfloat16
f32 = jnp.float32

CYCLES = {8: (0, 2, 4, 6, 7, 5, 3, 1)}


def dot(left, right, over_left, over_right):
    return lax.dot_general(
        left, right, (((over_left,), (over_right,)), ((), ())), preferred_element_type=f32
    )


def product(left, right):
    return dot(left, right, 1, 0)


def product_tn(left, right):
    return dot(left, right, 0, 0)


def product_nt(left, right):
    return dot(left, right, 1, 1)


def rms_norm(values, gain_vec):
    return values * lax.rsqrt(jnp.mean(values * values, axis=-1, keepdims=True) + 1e-06) * gain_vec


def short_conv(values, taps):
    total = values * taps[0]
    for shift in range(1, CONV_K):
        moved = jnp.concatenate(
            [jnp.zeros((shift, values.shape[1]), f32), values[:-shift]], axis=0
        )
        total = total + moved * taps[shift]
    return total


def front_part(inputs, g_one, taps):
    return short_conv(rms_norm(inputs, g_one), taps)


def head_parts(pack_ref, head, keep, in_window):
    query = pack_ref[:, FEAT * head : FEAT * (head + 1)].astype(low)
    key = pack_ref[:, LIN_G + FEAT * head : LIN_G + FEAT * (head + 1)].astype(low)
    start = 2 * LIN_G + VHEAD * head
    value = pack_ref[:, start : start + VHEAD].astype(low)
    start += WIN_G
    query_win = pack_ref[:, start : start + VHEAD].astype(low)
    start += WIN_G
    key_win = pack_ref[:, start : start + VHEAD].astype(low)
    scores = product_nt(query, key) * FEAT**-0.5
    kernel = jnp.where(keep, 1.0 + scores + 0.5 * scores * scores, 0.0)
    over = 1.0 / jnp.sum(kernel, axis=1, keepdims=True)
    share = kernel * over
    logits = jnp.where(in_window, product_nt(query_win, key_win) * VHEAD**-0.5, -1e30)
    raised = jnp.exp(logits - jnp.max(logits, axis=1, keepdims=True))
    probs = raised * (1.0 / jnp.sum(raised, axis=1, keepdims=True))
    return query, key, value, query_win, key_win, scores, over, share, probs


def masks(length, count):
    row = lax.broadcasted_iota(jnp.int32, (count, count), 0)
    col = lax.broadcasted_iota(jnp.int32, (count, count), 1)
    keep = (row >= col) & (col < length)
    return keep, keep & (row - col < WINDOW)


def mix_kernel(lens_ref, pack_ref, mixed_ref):
    keep, in_window = masks(lens_ref[pl.program_id(0)], pack_ref.shape[0])
    for head in range(HEADS_G):
        parts = head_parts(pack_ref, head, keep, in_window)
        value, share, probs = parts[2], parts[7], parts[8]
        out = product((share + probs).astype(low), value)
        mixed_ref[:, VHEAD * head : VHEAD * (head + 1)] = out.astype(low)


def mix_back_kernel(lens_ref, pack_ref, grad_ref, out_ref):
    keep, in_window = masks(lens_ref[pl.program_id(0)], pack_ref.shape[0])
    grad_query, grad_key = [], []
    for head in range(HEADS_G):
        query, key, value, query_win, key_win, scores, over, share, probs = head_parts(
            pack_ref, head, keep, in_window
        )
        grad = grad_ref[:, VHEAD * head : VHEAD * (head + 1)]
        weights = product_nt(grad, value)
        grad_raw = probs * (weights - jnp.sum(weights * probs, axis=1, keepdims=True))
        grad_raw = (grad_raw * VHEAD**-0.5).astype(low)
        centred = weights - jnp.sum(weights * share, axis=1, keepdims=True)
        grad_scores = jnp.where(keep, centred * (over * FEAT**-0.5) * (1.0 + scores), 0.0)
        grad_scores = grad_scores.astype(low)
        start = 2 * LIN_G + VHEAD * head
        out_ref[:, start : start + VHEAD] = product_tn((share + probs).astype(low), grad).astype(low)
        start += WIN_G
        out_ref[:, start : start + VHEAD] = product(grad_raw, key_win).astype(low)
        start += WIN_G
        out_ref[:, start : start + VHEAD] = product_tn(grad_raw, query_win).astype(low)
        grad_query.append(product(grad_scores, key).astype(low))
        grad_key.append(product_tn(grad_scores, query).astype(low))
    out_ref[:, : 2 * LIN_G] = jnp.concatenate(grad_query + grad_key, axis=1)


def per_sequence(body, name, count, widths, out_width, out_type, lens, *arrays):
    return pl.pallas_call(
        body,
        grid=(GROUP,),
        in_specs=[pl.BlockSpec(memory_space=pltpu.SMEM)]
        + [pl.BlockSpec((count, width), lambda i: (i, 0)) for width in widths],
        out_specs=pl.BlockSpec((count, out_width), lambda i: (i, 0)),
        out_shape=jax.ShapeDtypeStruct((GROUP * count, out_width), out_type),
        compiler_params=pltpu.CompilerParams(vmem_limit_bytes=32 * 1024 * 1024),
        cost_estimate=pl.CostEstimate(
            flops=2_000_000_000, bytes_accessed=10_000_000, transcendentals=1_000_000
        ),
        name=name,
    )(lens, *arrays)


bar = lax.optimization_barrier


def swap(value, over):
    return lax.ppermute(value, "grp", [(i, i ^ over) for i in range(GROUP)])


def group_gather(own, between=lambda: None):
    across = swap(own, 2)
    token = between()
    if token is not None:
        across = after(token, across)[0]
    count = own.shape[0]
    got = swap(jnp.concatenate([own, across]), 1)
    return jnp.concatenate([own, got[:count], across, got[count:]])


def reorder(stack):
    me = lax.axis_index("grp")
    return jnp.concatenate([lax.dynamic_slice_in_dim(stack, me ^ r, 1) for r in range(GROUP)])


def after(token, *values):
    return bar((*values, token))[:-1]


def steps_of(axis, size):
    step = 1
    while step < size:
        yield axis, size, step
        step *= 2


def everywhere(value, wide_size):
    stack = value[None]
    for axis, size, step in list(steps_of("wide", wide_size)) + list(steps_of("grp", GROUP)):
        other = lax.ppermute(stack, axis, [(i, i ^ step) for i in range(size)])
        upper = (lax.axis_index(axis) & step) > 0
        stack = jnp.where(
            upper, jnp.concatenate([other, stack], 0), jnp.concatenate([stack, other], 0)
        )
    return stack


def sum_everywhere(value, wide_size):
    for axis, size, step in list(steps_of("grp", GROUP)) + list(steps_of("wide", wide_size)):
        value = value + lax.ppermute(value, axis, [(i, i ^ step) for i in range(size)])
    return value


SMEM = pl.BlockSpec(memory_space=pltpu.SMEM)
VMEM = pl.BlockSpec(memory_space=pltpu.VMEM)
ANY = pl.BlockSpec(memory_space=pl.ANY)


def params(mib):
    return pltpu.CompilerParams(vmem_limit_bytes=mib * 1024 * 1024)


def cost(nbytes, flops=0):
    return pl.CostEstimate(flops=flops, bytes_accessed=nbytes, transcendentals=0)


def split_mixer(table, weights):
    rows = weights[0].shape[0]

    def body(table_ref, *refs):
        out = refs[-1]
        for j in range(GROUP):
            pieces = []
            for ref in refs[:-1]:
                width = ref.shape[1] // GROUP
                pieces.append(ref[:, j * width : (j + 1) * width].astype(low))
            out[j ^ table_ref[0]] = jnp.concatenate(pieces, axis=1)

    return pl.pallas_call(
        body,
        in_specs=[SMEM] + [VMEM] * len(weights),
        out_specs=VMEM,
        out_shape=jax.ShapeDtypeStruct((GROUP, rows, PACK), low),
        compiler_params=params(24),
        cost_estimate=cost(rows * PACK * GROUP * 6),
        name="split_mixer",
    )(table, *weights)


def split_gate_up(table, w_gate, w_up, wide_size, part, part_p):
    rows = w_gate.shape[0]
    hid_p = wide_size * part_p

    def body(table_ref, gate_ref, up_ref, out):
        fill = jnp.zeros((rows, part_p - part), f32)
        for j in range(GROUP):
            pieces = []
            for ref in (gate_ref, up_ref):
                for w in range(wide_size):
                    start = (j * wide_size + w) * part
                    pieces += [ref[:, start : start + part], fill]
            out[j ^ table_ref[0]] = jnp.concatenate(pieces, axis=1).astype(low)

    return pl.pallas_call(
        body,
        in_specs=[SMEM, VMEM, VMEM],
        out_specs=VMEM,
        out_shape=jax.ShapeDtypeStruct((GROUP, rows, 2 * hid_p), low),
        compiler_params=params(24),
        cost_estimate=cost(rows * hid_p * GROUP * 12),
        name="split_gate_up",
    )(table, w_gate, w_up)


def merge_gate_up(table, pieces, wide_size, part, part_p):
    rows = pieces[0].shape[0]
    hid_p = wide_size * part_p
    full = jax.ShapeDtypeStruct((rows, GROUP * wide_size * part), f32)

    def body(table_ref, a, b, c, d, gate_ref, up_ref, held):
        for r, ref in enumerate((a, b, c, d)):
            held[r] = ref[...].astype(f32)
        for at, out in ((0, gate_ref), (hid_p, up_ref)):
            for j in range(GROUP):
                block = held[j ^ table_ref[0]]
                parts = [block[:, at + w * part_p : at + w * part_p + part] for w in range(wide_size)]
                start = j * wide_size * part
                out[:, start : start + wide_size * part] = jnp.concatenate(parts, axis=1)

    return pl.pallas_call(
        body,
        in_specs=[SMEM] + [VMEM] * 4,
        out_specs=[VMEM, VMEM],
        out_shape=[full, full],
        scratch_shapes=[pltpu.VMEM((GROUP, rows, 2 * hid_p), f32)],
        compiler_params=params(24),
        cost_estimate=cost(rows * hid_p * GROUP * 12),
        name="merge_gate_up",
    )(table, *pieces)


def merge_mixer(table, pieces):
    rows = pieces[0].shape[0]
    widths = [LIN_G, LIN_G, WIN_G, WIN_G, WIN_G]

    def body(table_ref, a, b, c, d, *refs):
        outs, held = refs[:-1], refs[-1]
        for r, ref in enumerate((a, b, c, d)):
            held[r] = ref[...].astype(f32)
        blocks = [held[j ^ table_ref[0]] for j in range(GROUP)]
        at = 0
        for width, out in zip(widths, outs):
            out[...] = jnp.concatenate([block[:, at : at + width] for block in blocks], axis=1)
            at += width

    return pl.pallas_call(
        body,
        in_specs=[SMEM] + [VMEM] * 4,
        out_specs=[VMEM] * 5,
        out_shape=[jax.ShapeDtypeStruct((rows, GROUP * width), f32) for width in widths],
        scratch_shapes=[pltpu.VMEM((GROUP, rows, PACK), f32)],
        compiler_params=params(24),
        cost_estimate=cost(rows * PACK * GROUP * 6),
        name="merge_mixer",
    )(table, *pieces)


def place(table, ways, grouped, size):
    piece = ways[0][0]
    rows, width = piece.shape[-2:]
    shape = (GROUP, size, rows, width) if grouped else (size, rows, 2 * width)

    def body(table_ref, *refs):
        out, sems = refs[-2:]
        copies = []
        for d in (0, 1):
            for s in range(size):
                ref = refs[d * size + s]
                owner = table_ref[1 + d * size + s]
                if grouped:
                    for i in range(2):
                        copies.append((ref.at[i], out.at[(2 * d + i) ^ table_ref[0], owner]))
                else:
                    copies.append((ref, out.at[owner, :, d * width : (d + 1) * width]))
        copies = [pltpu.make_async_copy(of, to, sems.at[k]) for k, (of, to) in enumerate(copies)]
        for copy in copies:
            copy.start()
        for copy in copies:
            copy.wait()

    return pl.pallas_call(
        body,
        in_specs=[SMEM] + [ANY] * (2 * size),
        out_specs=ANY,
        out_shape=jax.ShapeDtypeStruct(shape, low),
        scratch_shapes=[pltpu.SemaphoreType.DMA(((4 if grouped else 2) * size,))],
        compiler_params=params(2),
        cost_estimate=cost(8 * size * rows * width * piece.ndim),
        name="place",
    )(table, *ways[0], *ways[1])


def pick_add(table, terms, got, step, size, keep_rows=None):
    grouped = terms.ndim == 4
    rows, width = terms.shape[-2:]
    k = (step + 1) % size
    if not grouped:
        width //= 2

    def body(table_ref, *refs):
        mine, outs = refs[:2], refs[-2:] if keep_rows is None else refs[-1:]
        for d in (0, 1):
            total = mine[d][...].reshape(rows, width).astype(f32)
            if got is not None:
                total = total + refs[2 + d][...].reshape(rows, width).astype(f32)
            if keep_rows is None:
                outs[d][...] = total.reshape(outs[d].shape).astype(low)
            else:
                outs[0][:, d * width : (d + 1) * width] = total[:keep_rows]

    def owner(table_ref, d):
        return table_ref[1 + d * size + k]

    if grouped:
        grid = (2,)
        term_specs = [
            pl.BlockSpec(
                (1, 1, rows, width),
                lambda i, t, d=d: ((2 * d + i) ^ t[0], owner(t, d), 0, 0),
            )
            for d in (0, 1)
        ]
        piece = pl.BlockSpec((1, rows, width), lambda i, t: (i, 0, 0))
        shape = jax.ShapeDtypeStruct((2, rows, width), low)
    else:
        grid = (1,)
        term_specs = [
            pl.BlockSpec((1, rows, width), lambda i, t, d=d: (owner(t, d), 0, d)) for d in (0, 1)
        ]
        piece = pl.BlockSpec((rows, width), lambda i, t: (0, 0))
        shape = jax.ShapeDtypeStruct((rows, width), low)
    out_specs, out_shape = [piece, piece], [shape, shape]
    if keep_rows is not None:
        out_specs = [pl.BlockSpec((keep_rows, 2 * width), lambda i, t: (0, 0))]
        out_shape = [jax.ShapeDtypeStruct((keep_rows, 2 * width), f32)]
    came = [] if got is None else list(got)

    return pl.pallas_call(
        body,
        grid_spec=pltpu.PrefetchScalarGridSpec(
            num_scalar_prefetch=1,
            grid=grid,
            in_specs=term_specs + [piece] * len(came),
            out_specs=out_specs,
        ),
        out_shape=out_shape,
        compiler_params=params(16),
        cost_estimate=cost(8 * rows * width * 3),
        name="pick_add",
    )(table, terms, terms, *came)


def round_ring(cycle, d):
    size = len(cycle)
    way = [(cycle[i], cycle[(i + 1) % size]) for i in range(size)]
    return way if d == 0 else [(to, of) for of, to in way]


class GatherRing:
    def __init__(self, halves, grouped, size, table):
        self.held = [[half] for half in halves]
        self.grouped, self.size, self.table = grouped, size, table
        self.steps = size - 1 if size in CYCLES else 0

    def step(self, token=None):
        if self.steps == 0:
            return
        self.steps -= 1
        for d, held in enumerate(self.held):
            value = held[-1] if token is None else after(token, held[-1])[0]
            held.append(lax.ppermute(value, "wide", round_ring(CYCLES[self.size], d)))

    def seen(self):
        return self.held[0][max(len(self.held[0]) - 2, 0)]

    def done(self, token=None):
        while self.steps:
            self.step()
        if self.size in CYCLES:
            ways = self.held
            if token is not None:
                ways = [list(after(token, *held)) for held in ways]
            out = place(self.table, ways, self.grouped, self.size)
        elif self.grouped:
            block = jnp.concatenate([self.held[0][0], self.held[1][0]], axis=0)
            out = jnp.moveaxis(lax.all_gather(block, "wide"), 0, 1)
            out = reorder(out)
        else:
            block = jnp.concatenate([self.held[0][0], self.held[1][0]], axis=1)
            out = lax.all_gather(block, "wide")
        return out.reshape(-1, out.shape[-1])


class SumRing:
    def __init__(self, terms, size, table, keep_rows=None):
        self.terms, self.size, self.table, self.keep_rows = terms, size, table, keep_rows
        self.at, self.got, self.last = 0, None, terms
        self.left = size - 1 if size in CYCLES else 0

    def step(self, token=None):
        if self.left == 0:
            return
        self.left -= 1
        got = self.got
        if token is not None:
            got = after(token, *got) if got is not None else None
            if got is None:
                self.terms = after(token, self.terms)[0]
        sums = pick_add(self.table, self.terms, got, self.at, self.size)
        self.last = sums[0]
        self.at += 1
        cycle = CYCLES[self.size]
        self.got = [lax.ppermute(sums[d], "wide", round_ring(cycle, d)) for d in (0, 1)]

    def done(self, token=None):
        while self.left:
            self.step()
        if self.size in CYCLES:
            got = self.got if token is None else after(token, *self.got)
            out = pick_add(self.table, self.terms, got, self.at, self.size, self.keep_rows)
            return out if self.keep_rows is None else out[0]
        if self.keep_rows is None:
            full = lax.psum_scatter(
                self.terms.astype(f32), "wide", scatter_dimension=1, tiled=True
            )[:, 0]
            full = reorder(full).astype(low)
            return full[:2], full[2:]
        full = lax.psum_scatter(self.terms.astype(f32), "wide", scatter_dimension=0, tiled=True)
        return full[0, : self.keep_rows]


def table_of(wide_size):
    me = lax.axis_index("grp").astype(jnp.int32)
    if wide_size not in CYCLES:
        return me[None]
    cycle = CYCLES[wide_size]
    rows = []
    for w in range(wide_size):
        at = cycle.index(w)
        rows.append(
            [cycle[(at - s) % wide_size] for s in range(wide_size)]
            + [cycle[(at + s) % wide_size] for s in range(wide_size)]
        )
    row = lax.dynamic_index_in_dim(
        jnp.array(rows, jnp.int32), lax.axis_index("wide"), 0, keepdims=False
    )
    return jnp.concatenate([me[None], row])


def shards(
    tokens,
    lengths,
    cotangent,
    norm_gain,
    conv_weight,
    w_query,
    w_key,
    w_value,
    w_query_window,
    w_key_window,
    w_out,
    ffn_gain,
    w_gate,
    w_up,
    w_down,
    *,
    wide_size,
):
    me = lax.axis_index("grp")
    spot = me * wide_size + lax.axis_index("wide")
    count = tokens.shape[0]
    rows = w_query.shape[0]
    part = w_down.shape[0]
    part_p = -(-part // 16) * 16
    hid_p = wide_size * part_p
    length = lengths[0]
    is_valid = (jnp.arange(count, dtype=jnp.int32) < length).astype(f32)
    table = table_of(wide_size)

    small = jnp.concatenate(
        [
            norm_gain[None],
            conv_weight.T,
            ffn_gain[None],
            jnp.broadcast_to(length.astype(f32), (1, rows)),
            jnp.zeros((2, rows), f32),
        ],
        axis=0,
    ).astype(low)
    small_all = everywhere(small, wide_size)

    half = D // 2
    out_low = w_out.astype(low)
    out_ring = GatherRing([out_low[:, :half], out_low[:, half:]], False, wide_size, table)
    mixer_blocks = split_mixer(table, (w_query, w_key, w_value, w_query_window, w_key_window))
    mixer_got = [mixer_blocks[0]] + [swap(mixer_blocks[r], r) for r in range(1, GROUP)]
    mix_ring = GatherRing(
        [jnp.stack(mixer_got[:2]), jnp.stack(mixer_got[2:])], True, wide_size, table
    )
    gu_blocks = split_gate_up(table, w_gate, w_up, wide_size, part, part_p)
    gu_blocks = after(mixer_got[3], gu_blocks)[0]
    gu_got = [gu_blocks[0]] + [swap(gu_blocks[r], r) for r in range(1, GROUP)]
    gu_ring = GatherRing([jnp.stack(gu_got[:2]), jnp.stack(gu_got[2:])], True, wide_size, table)
    down_low = jnp.pad(w_down.astype(low), ((0, part_p - part), (0, 0)))
    down_ring = GatherRing([down_low[:, :half], down_low[:, half:]], False, wide_size, table)

    g_one, tap_0, tap_1, tap_2, g_two = [
        small_all[:, i].reshape(D).astype(f32) for i in range(5)
    ]
    taps = jnp.stack([tap_0, tap_1, tap_2])
    group_lens = small_all[:, 5, 0].astype(jnp.int32).reshape(GROUP, wide_size)
    group_lens = lax.dynamic_index_in_dim(group_lens, lax.axis_index("wide"), 1, keepdims=False)
    group_lens = reorder(group_lens)

    inputs = tokens.astype(f32)
    conv_out, front_pull = jax.vjp(front_part, inputs, g_one, taps)
    conv_low = group_gather(conv_out.astype(low))
    grad_outer = cotangent.astype(f32) * is_valid[:, None]
    down_own = after(conv_low, grad_outer.astype(low))[0]
    down_in = group_gather(down_own)

    for _ in range(3):
        out_ring.step()
    for k in range(7):
        mix_ring.step()
        out_ring.step()
        if k == 4:
            gu_ring.step(mix_ring.seen())
    gu_ring.step(mix_ring.held[0][-1])
    w_mix = mix_ring.done()
    wo = out_ring.done()

    def advance(token, *rings):
        for ring in rings:
            ring.step(token)

    pack = product(conv_low, w_mix)
    advance(pack, gu_ring)
    mixed = per_sequence(
        mix_kernel, "mix", count, (PACK,), WIN_G, low, group_lens, pack
    )
    advance(mixed, gu_ring)

    def partial_sum(make, between=lambda across: ()):
        far = make(1).astype(low)
        over = swap(far[count:], 1)
        near = make(0).astype(low)
        peer = swap(near[count:], 1)
        across = (far[:count].astype(f32) + over.astype(f32)).astype(low)
        got = swap(across, 2)
        for token in between(across):
            got = after(token, got)[0]
        return near[:count].astype(f32) + peer.astype(f32) + got.astype(f32)

    def rows_of(value, x):
        return value[2 * x * count : 2 * (x + 1) * count]

    def in_forward(across):
        advance(across, gu_ring)
        advance(gu_ring.seen(), gu_ring)
        return [gu_ring.seen()]

    resid = inputs + partial_sum(lambda x: product(rows_of(mixed, x), wo), in_forward)
    normed_f, middle_pull = jax.vjp(rms_norm, resid, g_two)
    normed_own = normed_f.astype(low)
    advance(normed_own, gu_ring)

    def in_gather():
        down_ring.step(gu_ring.seen())
        down_ring.step()
        return down_ring.seen()

    normed = group_gather(normed_own, in_gather)
    w_gu = gu_ring.done(down_ring.seen())
    down_ring.step(w_gu)
    gate_up = product(*after(down_ring.seen(), normed, w_gu))
    advance(gate_up, down_ring)
    gate_pre, up_pre = gate_up[:, :hid_p], gate_up[:, hid_p:]
    sigma = jax.nn.sigmoid(gate_pre)
    silu_gate = gate_pre * sigma
    hidden = bar((silu_gate * up_pre).astype(low))
    advance(hidden, down_ring)

    grad_down = product_tn(*after(down_ring.seen(), hidden, down_in)).astype(low)
    advance(grad_down, down_ring)
    down_sum = SumRing(grad_down.reshape(wide_size, part_p, D), wide_size, table, part)
    down_sum.step()
    down_ring.step(down_sum.last)
    wd = down_ring.done()
    grad_hidden = product_nt(down_in, wd).astype(low).astype(f32)
    grad_gu = jnp.concatenate(
        [
            (grad_hidden * up_pre * sigma * (1.0 + gate_pre * (1.0 - sigma))).astype(low),
            (grad_hidden * silu_gate).astype(low),
        ],
        axis=1,
    )
    grad_gu = bar(grad_gu)
    down_sum.step(grad_gu)
    sums = []

    def in_backward(across):
        down_sum.step(across)
        grad_w_gu = product_tn(*after((across, down_sum.last), normed, grad_gu)).astype(low)
        gu_sum = SumRing(grad_w_gu.reshape(GROUP, wide_size, rows, 2 * hid_p), wide_size, table)
        gu_sum.step()
        down_sum.step(gu_sum.last)
        gu_sum.step(down_sum.last)
        sums.append(gu_sum)
        return [gu_sum.last]

    grad_normed = partial_sum(lambda x: product_nt(rows_of(grad_gu, x), w_gu), in_backward)
    gu_sum = sums[0]
    grad_resid_norm, grad_ffn_gain = middle_pull(grad_normed.astype(low).astype(f32))
    grad_resid = grad_outer + grad_resid_norm
    branch_own = grad_resid.astype(low)
    advance(branch_own, down_sum)

    def in_branch():
        gu_sum.step(down_sum.last)
        return gu_sum.last

    branch_in = group_gather(branch_own, in_branch)
    down_sum.step(branch_in)
    grad_mixed = product_nt(branch_in, wo).astype(low)
    advance(grad_mixed, gu_sum)
    grad_mixed = after(gu_sum.last, grad_mixed)[0]
    grad_pack = per_sequence(
        mix_back_kernel, "mix_back", count, (PACK, WIN_G), PACK, low, group_lens, pack, grad_mixed
    )
    advance(grad_pack, gu_sum)
    grad_w_down = down_sum.done(grad_pack)
    grad_mix = product_tn(*after(gu_sum.last, conv_low, grad_pack)).astype(low)
    mix_sum = SumRing(grad_mix.reshape(GROUP, wide_size, rows, PACK), wide_size, table)
    mix_sum.step()
    advance(mix_sum.last, gu_sum)
    grad_pack = after(gu_sum.last, grad_pack)[0]

    def in_front(across):
        advance(across, mix_sum, gu_sum)
        grad_out = product_tn(*after(gu_sum.last, mixed, branch_in)).astype(low)
        advance(grad_out, mix_sum)
        sums.append(grad_out)
        return [mix_sum.last]

    grad_conv_low = partial_sum(lambda x: product_nt(rows_of(grad_pack, x), w_mix), in_front)
    grad_out = sums[1]
    grad_front, grad_norm_gain, grad_taps = front_pull(grad_conv_low.astype(low).astype(f32))
    grad_tokens = (grad_resid + grad_front).astype(low)
    gu_halves = gu_sum.done(mix_sum.last)
    out_sum = SumRing(grad_out.reshape(wide_size, rows, D), wide_size, table, rows)
    out_sum.step(gu_halves[0])
    advance(gu_halves[0], mix_sum)

    def in_down(across):
        advance(across, mix_sum, out_sum)
        return []

    hidden_late = after(gu_halves[0], hidden)[0]
    down = partial_sum(lambda x: product(rows_of(hidden_late, x), wd), in_down)
    block_out = ((resid + down) * is_valid[:, None]).astype(low)

    def to_owner(halves):
        blocks = [halves[0][0], halves[0][1], halves[1][0], halves[1][1]]
        return [blocks[0]] + [swap(blocks[r], r) for r in range(1, GROUP)]

    mix_sum.step()
    out_sum.step()
    grad_gate, grad_up = merge_gate_up(table, to_owner(gu_halves), wide_size, part, part_p)
    advance(grad_gate, mix_sum, out_sum)
    grad_w_out = out_sum.done()
    mixer_grads = merge_mixer(table, to_owner(mix_sum.done()))
    gains = jnp.concatenate(
        [grad_norm_gain[None], grad_taps, grad_ffn_gain[None], jnp.zeros((3, D), f32)], axis=0
    )
    gains = sum_everywhere(gains, wide_size).reshape(8, GROUP * wide_size, rows)
    gains = lax.dynamic_index_in_dim(gains, spot, 1, keepdims=False)
    return (
        block_out,
        grad_tokens,
        gains[0],
        gains[1 : 1 + CONV_K].T,
        *mixer_grads,
        grad_w_out,
        gains[1 + CONV_K],
        grad_gate,
        grad_up,
        grad_w_down,
    )


def solution(mesh):
    rows = P(("grp", "wide"), None)
    flat = P(("grp", "wide"))
    return jax.shard_map(
        functools.partial(shards, wide_size=mesh.shape["wide"]),
        mesh=mesh,
        in_specs=(rows, flat, rows, flat, rows, rows, rows, rows, rows, rows, rows, flat, rows, rows, rows),
        out_specs=(rows, rows, flat, rows, rows, rows, rows, rows, rows, rows, flat, rows, rows, rows),
        check_vma=False,
    )
```

```python
import functools

import jax
import jax.numpy as jnp
from jax import lax
from jax.experimental import pallas as pl
from jax.experimental.pallas import tpu as pltpu
from jax.sharding import PartitionSpec as P

D = 2048
HEADS = 16
FEAT = 16
WINDOW = 64
CONV_K = 3
VHEAD = 128
GROUP = 4
HEADS_G = HEADS // GROUP
LIN_G = HEADS_G * FEAT
WIN_G = HEADS_G * VHEAD
PACK = 2 * LIN_G + 3 * WIN_G

low = jnp.bfloat16
f32 = jnp.float32

CYCLES = {8: (0, 2, 4, 6, 7, 5, 3, 1)}


def dot(left, right, over_left, over_right):
    return lax.dot_general(
        left, right, (((over_left,), (over_right,)), ((), ())), preferred_element_type=f32
    )


def product(left, right):
    return dot(left, right, 1, 0)


def product_tn(left, right):
    return dot(left, right, 0, 0)


def product_nt(left, right):
    return dot(left, right, 1, 1)


def rms_norm(values, gain_vec):
    return values * lax.rsqrt(jnp.mean(values * values, axis=-1, keepdims=True) + 1e-06) * gain_vec


def short_conv(values, taps):
    total = values * taps[0]
    for shift in range(1, CONV_K):
        moved = jnp.concatenate(
            [jnp.zeros((shift, values.shape[1]), f32), values[:-shift]], axis=0
        )
        total = total + moved * taps[shift]
    return total


def front_part(inputs, g_one, taps):
    return short_conv(rms_norm(inputs, g_one), taps)


def head_parts(pack_ref, head, keep, in_window):
    query = pack_ref[:, FEAT * head : FEAT * (head + 1)].astype(low)
    key = pack_ref[:, LIN_G + FEAT * head : LIN_G + FEAT * (head + 1)].astype(low)
    start = 2 * LIN_G + VHEAD * head
    value = pack_ref[:, start : start + VHEAD].astype(low)
    start += WIN_G
    query_win = pack_ref[:, start : start + VHEAD].astype(low)
    start += WIN_G
    key_win = pack_ref[:, start : start + VHEAD].astype(low)
    scores = product_nt(query, key) * FEAT**-0.5
    kernel = jnp.where(keep, 1.0 + scores + 0.5 * scores * scores, 0.0)
    over = 1.0 / jnp.sum(kernel, axis=1, keepdims=True)
    share = kernel * over
    logits = jnp.where(in_window, product_nt(query_win, key_win) * VHEAD**-0.5, -1e30)
    raised = jnp.exp(logits - jnp.max(logits, axis=1, keepdims=True))
    probs = raised * (1.0 / jnp.sum(raised, axis=1, keepdims=True))
    return query, key, value, query_win, key_win, scores, over, share, probs


def masks(length, count):
    row = lax.broadcasted_iota(jnp.int32, (count, count), 0)
    col = lax.broadcasted_iota(jnp.int32, (count, count), 1)
    keep = (row >= col) & (col < length)
    return keep, keep & (row - col < WINDOW)


def mix_kernel(lens_ref, pack_ref, mixed_ref):
    keep, in_window = masks(lens_ref[pl.program_id(0)], pack_ref.shape[0])
    for head in range(HEADS_G):
        parts = head_parts(pack_ref, head, keep, in_window)
        value, share, probs = parts[2], parts[7], parts[8]
        out = product((share + probs).astype(low), value)
        mixed_ref[:, VHEAD * head : VHEAD * (head + 1)] = out.astype(low)


def mix_back_kernel(lens_ref, pack_ref, grad_ref, out_ref):
    keep, in_window = masks(lens_ref[pl.program_id(0)], pack_ref.shape[0])
    grad_query, grad_key = [], []
    for head in range(HEADS_G):
        query, key, value, query_win, key_win, scores, over, share, probs = head_parts(
            pack_ref, head, keep, in_window
        )
        grad = grad_ref[:, VHEAD * head : VHEAD * (head + 1)]
        weights = product_nt(grad, value)
        grad_raw = probs * (weights - jnp.sum(weights * probs, axis=1, keepdims=True))
        grad_raw = (grad_raw * VHEAD**-0.5).astype(low)
        centred = weights - jnp.sum(weights * share, axis=1, keepdims=True)
        grad_scores = jnp.where(keep, centred * (over * FEAT**-0.5) * (1.0 + scores), 0.0)
        grad_scores = grad_scores.astype(low)
        start = 2 * LIN_G + VHEAD * head
        out_ref[:, start : start + VHEAD] = product_tn((share + probs).astype(low), grad).astype(low)
        start += WIN_G
        out_ref[:, start : start + VHEAD] = product(grad_raw, key_win).astype(low)
        start += WIN_G
        out_ref[:, start : start + VHEAD] = product_tn(grad_raw, query_win).astype(low)
        grad_query.append(product(grad_scores, key).astype(low))
        grad_key.append(product_tn(grad_scores, query).astype(low))
    out_ref[:, : 2 * LIN_G] = jnp.concatenate(grad_query + grad_key, axis=1)


def per_sequence(body, name, count, widths, out_width, out_type, lens, *arrays):
    return pl.pallas_call(
        body,
        grid=(GROUP,),
        in_specs=[pl.BlockSpec(memory_space=pltpu.SMEM)]
        + [pl.BlockSpec((count, width), lambda i: (i, 0)) for width in widths],
        out_specs=pl.BlockSpec((count, out_width), lambda i: (i, 0)),
        out_shape=jax.ShapeDtypeStruct((GROUP * count, out_width), out_type),
        compiler_params=pltpu.CompilerParams(vmem_limit_bytes=32 * 1024 * 1024),
        cost_estimate=pl.CostEstimate(
            flops=2_000_000_000, bytes_accessed=10_000_000, transcendentals=1_000_000
        ),
        name=name,
    )(lens, *arrays)


bar = lax.optimization_barrier


def swap(value, over):
    return lax.ppermute(value, "grp", [(i, i ^ over) for i in range(GROUP)])


def group_gather(own, between=lambda: None):
    across = swap(own, 2)
    token = between()
    if token is not None:
        across = after(token, across)[0]
    count = own.shape[0]
    got = swap(jnp.concatenate([own, across]), 1)
    return jnp.concatenate([own, got[:count], across, got[count:]])


def reorder(stack):
    me = lax.axis_index("grp")
    return jnp.concatenate([lax.dynamic_slice_in_dim(stack, me ^ r, 1) for r in range(GROUP)])


def after(token, *values):
    return bar((*values, token))[:-1]


def steps_of(axis, size):
    step = 1
    while step < size:
        yield axis, size, step
        step *= 2


def everywhere(value, wide_size):
    stack = value[None]
    for axis, size, step in list(steps_of("wide", wide_size)) + list(steps_of("grp", GROUP)):
        other = lax.ppermute(stack, axis, [(i, i ^ step) for i in range(size)])
        upper = (lax.axis_index(axis) & step) > 0
        stack = jnp.where(
            upper, jnp.concatenate([other, stack], 0), jnp.concatenate([stack, other], 0)
        )
    return stack


def sum_everywhere(value, wide_size, tokens):
    for k, (axis, size, step) in enumerate(
        list(steps_of("grp", GROUP)) + list(steps_of("wide", wide_size))
    ):
        got = lax.ppermute(value, axis, [(i, i ^ step) for i in range(size)])
        value = value + (after(tokens[k], got)[0] if k < len(tokens) else got)
    return value


SMEM = pl.BlockSpec(memory_space=pltpu.SMEM)
VMEM = pl.BlockSpec(memory_space=pltpu.VMEM)
ANY = pl.BlockSpec(memory_space=pl.ANY)


def params(mib):
    return pltpu.CompilerParams(vmem_limit_bytes=mib * 1024 * 1024)


def cost(nbytes, flops=0):
    return pl.CostEstimate(flops=flops, bytes_accessed=nbytes, transcendentals=0)


def split_mixer(table, weights):
    rows = weights[0].shape[0]

    def body(table_ref, *refs):
        out = refs[-1]
        for j in range(GROUP):
            pieces = []
            for ref in refs[:-1]:
                width = ref.shape[1] // GROUP
                pieces.append(ref[:, j * width : (j + 1) * width].astype(low))
            out[j ^ table_ref[0]] = jnp.concatenate(pieces, axis=1)

    return pl.pallas_call(
        body,
        in_specs=[SMEM] + [VMEM] * len(weights),
        out_specs=VMEM,
        out_shape=jax.ShapeDtypeStruct((GROUP, rows, PACK), low),
        compiler_params=params(24),
        cost_estimate=cost(rows * PACK * GROUP * 6),
        name="split_mixer",
    )(table, *weights)


def split_gate_up(table, w_gate, w_up, wide_size, part, part_p):
    rows = w_gate.shape[0]
    hid_p = wide_size * part_p

    def body(table_ref, gate_ref, up_ref, out):
        fill = jnp.zeros((rows, part_p - part), f32)
        for j in range(GROUP):
            pieces = []
            for ref in (gate_ref, up_ref):
                for w in range(wide_size):
                    start = (j * wide_size + w) * part
                    pieces += [ref[:, start : start + part], fill]
            out[j ^ table_ref[0]] = jnp.concatenate(pieces, axis=1).astype(low)

    return pl.pallas_call(
        body,
        in_specs=[SMEM, VMEM, VMEM],
        out_specs=VMEM,
        out_shape=jax.ShapeDtypeStruct((GROUP, rows, 2 * hid_p), low),
        compiler_params=params(24),
        cost_estimate=cost(rows * hid_p * GROUP * 12),
        name="split_gate_up",
    )(table, w_gate, w_up)


def merge_gate_up(table, pieces, wide_size, part, part_p):
    rows = pieces[0].shape[0]
    hid_p = wide_size * part_p
    full = jax.ShapeDtypeStruct((rows, GROUP * wide_size * part), f32)

    def body(table_ref, a, b, c, d, gate_ref, up_ref, held):
        for r, ref in enumerate((a, b, c, d)):
            held[r] = ref[...].astype(f32)
        for at, out in ((0, gate_ref), (hid_p, up_ref)):
            for j in range(GROUP):
                block = held[j ^ table_ref[0]]
                parts = [block[:, at + w * part_p : at + w * part_p + part] for w in range(wide_size)]
                start = j * wide_size * part
                out[:, start : start + wide_size * part] = jnp.concatenate(parts, axis=1)

    return pl.pallas_call(
        body,
        in_specs=[SMEM] + [VMEM] * 4,
        out_specs=[VMEM, VMEM],
        out_shape=[full, full],
        scratch_shapes=[pltpu.VMEM((GROUP, rows, 2 * hid_p), f32)],
        compiler_params=params(24),
        cost_estimate=cost(rows * hid_p * GROUP * 12),
        name="merge_gate_up",
    )(table, *pieces)


def merge_mixer(table, pieces):
    rows = pieces[0].shape[0]
    widths = [LIN_G, LIN_G, WIN_G, WIN_G, WIN_G]

    def body(table_ref, a, b, c, d, *refs):
        outs, held = refs[:-1], refs[-1]
        for r, ref in enumerate((a, b, c, d)):
            held[r] = ref[...].astype(f32)
        blocks = [held[j ^ table_ref[0]] for j in range(GROUP)]
        at = 0
        for width, out in zip(widths, outs):
            out[...] = jnp.concatenate([block[:, at : at + width] for block in blocks], axis=1)
            at += width

    return pl.pallas_call(
        body,
        in_specs=[SMEM] + [VMEM] * 4,
        out_specs=[VMEM] * 5,
        out_shape=[jax.ShapeDtypeStruct((rows, GROUP * width), f32) for width in widths],
        scratch_shapes=[pltpu.VMEM((GROUP, rows, PACK), f32)],
        compiler_params=params(24),
        cost_estimate=cost(rows * PACK * GROUP * 6),
        name="merge_mixer",
    )(table, *pieces)


def place(table, ways, grouped, size):
    piece = ways[0][0]
    rows, width = piece.shape[-2:]
    shape = (GROUP, size, rows, width) if grouped else (size, rows, 2 * width)

    def body(table_ref, *refs):
        out, sems = refs[-2:]
        copies = []
        for d in (0, 1):
            for s in range(size):
                ref = refs[d * size + s]
                owner = table_ref[1 + d * size + s]
                if grouped:
                    for i in range(2):
                        copies.append((ref.at[i], out.at[(2 * d + i) ^ table_ref[0], owner]))
                else:
                    copies.append((ref, out.at[owner, :, d * width : (d + 1) * width]))
        copies = [pltpu.make_async_copy(of, to, sems.at[k]) for k, (of, to) in enumerate(copies)]
        for copy in copies:
            copy.start()
        for copy in copies:
            copy.wait()

    return pl.pallas_call(
        body,
        in_specs=[SMEM] + [ANY] * (2 * size),
        out_specs=ANY,
        out_shape=jax.ShapeDtypeStruct(shape, low),
        scratch_shapes=[pltpu.SemaphoreType.DMA(((4 if grouped else 2) * size,))],
        compiler_params=params(2),
        cost_estimate=cost(8 * size * rows * width * piece.ndim),
        name="place",
    )(table, *ways[0], *ways[1])


def pick_add(table, terms, got, step, size, keep_rows=None):
    grouped = terms.ndim == 4
    rows, width = terms.shape[-2:]
    k = (step + 1) % size
    if not grouped:
        width //= 2

    def body(table_ref, *refs):
        mine, outs = refs[:2], refs[-2:] if keep_rows is None else refs[-1:]
        for d in (0, 1):
            total = mine[d][...].reshape(rows, width).astype(f32)
            if got is not None:
                total = total + refs[2 + d][...].reshape(rows, width).astype(f32)
            if keep_rows is None:
                outs[d][...] = total.reshape(outs[d].shape).astype(low)
            else:
                outs[0][:, d * width : (d + 1) * width] = total[:keep_rows]

    def owner(table_ref, d):
        return table_ref[1 + d * size + k]

    if grouped:
        grid = (2,)
        term_specs = [
            pl.BlockSpec(
                (1, 1, rows, width),
                lambda i, t, d=d: ((2 * d + i) ^ t[0], owner(t, d), 0, 0),
            )
            for d in (0, 1)
        ]
        piece = pl.BlockSpec((1, rows, width), lambda i, t: (i, 0, 0))
        shape = jax.ShapeDtypeStruct((2, rows, width), low)
    else:
        grid = (1,)
        term_specs = [
            pl.BlockSpec((1, rows, width), lambda i, t, d=d: (owner(t, d), 0, d)) for d in (0, 1)
        ]
        piece = pl.BlockSpec((rows, width), lambda i, t: (0, 0))
        shape = jax.ShapeDtypeStruct((rows, width), low)
    out_specs, out_shape = [piece, piece], [shape, shape]
    if keep_rows is not None:
        out_specs = [pl.BlockSpec((keep_rows, 2 * width), lambda i, t: (0, 0))]
        out_shape = [jax.ShapeDtypeStruct((keep_rows, 2 * width), f32)]
    came = [] if got is None else list(got)

    return pl.pallas_call(
        body,
        grid_spec=pltpu.PrefetchScalarGridSpec(
            num_scalar_prefetch=1,
            grid=grid,
            in_specs=term_specs + [piece] * len(came),
            out_specs=out_specs,
        ),
        out_shape=out_shape,
        compiler_params=params(16),
        cost_estimate=cost(8 * rows * width * 3),
        name="pick_add",
    )(table, terms, terms, *came)


def round_ring(cycle, d):
    size = len(cycle)
    way = [(cycle[i], cycle[(i + 1) % size]) for i in range(size)]
    return way if d == 0 else [(to, of) for of, to in way]


class GatherRing:
    def __init__(self, halves, grouped, size, table):
        self.held = [[half] for half in halves]
        self.grouped, self.size, self.table = grouped, size, table
        self.steps = size - 1 if size in CYCLES else 0

    def step(self, token=None):
        if self.steps == 0:
            return
        self.steps -= 1
        for d, held in enumerate(self.held):
            value = held[-1] if token is None else after(token, held[-1])[0]
            held.append(lax.ppermute(value, "wide", round_ring(CYCLES[self.size], d)))

    def seen(self):
        return self.held[0][max(len(self.held[0]) - 2, 0)]

    def done(self, token=None):
        while self.steps:
            self.step()
        if self.size in CYCLES:
            ways = self.held
            if token is not None:
                ways = [list(after(token, *held)) for held in ways]
            out = place(self.table, ways, self.grouped, self.size)
        elif self.grouped:
            block = jnp.concatenate([self.held[0][0], self.held[1][0]], axis=0)
            out = jnp.moveaxis(lax.all_gather(block, "wide"), 0, 1)
            out = reorder(out)
        else:
            block = jnp.concatenate([self.held[0][0], self.held[1][0]], axis=1)
            out = lax.all_gather(block, "wide")
        return out.reshape(-1, out.shape[-1])


class SumRing:
    def __init__(self, terms, size, table, keep_rows=None):
        self.terms, self.size, self.table, self.keep_rows = terms, size, table, keep_rows
        self.at, self.got, self.last = 0, None, terms
        self.left = size - 1 if size in CYCLES else 0

    def step(self, token=None):
        if self.left == 0:
            return
        self.left -= 1
        got = self.got
        if token is not None:
            got = after(token, *got) if got is not None else None
            if got is None:
                self.terms = after(token, self.terms)[0]
        sums = pick_add(self.table, self.terms, got, self.at, self.size)
        self.last = sums[0]
        self.at += 1
        cycle = CYCLES[self.size]
        self.got = [lax.ppermute(sums[d], "wide", round_ring(cycle, d)) for d in (0, 1)]

    def done(self, token=None):
        while self.left:
            self.step()
        if self.size in CYCLES:
            got = self.got if token is None else after(token, *self.got)
            out = pick_add(self.table, self.terms, got, self.at, self.size, self.keep_rows)
            return out if self.keep_rows is None else out[0]
        if self.keep_rows is None:
            full = lax.psum_scatter(
                self.terms.astype(f32), "wide", scatter_dimension=1, tiled=True
            )[:, 0]
            full = reorder(full).astype(low)
            return full[:2], full[2:]
        full = lax.psum_scatter(self.terms.astype(f32), "wide", scatter_dimension=0, tiled=True)
        return full[0, : self.keep_rows]


def table_of(wide_size):
    me = lax.axis_index("grp").astype(jnp.int32)
    if wide_size not in CYCLES:
        return me[None]
    cycle = CYCLES[wide_size]
    rows = []
    for w in range(wide_size):
        at = cycle.index(w)
        rows.append(
            [cycle[(at - s) % wide_size] for s in range(wide_size)]
            + [cycle[(at + s) % wide_size] for s in range(wide_size)]
        )
    row = lax.dynamic_index_in_dim(
        jnp.array(rows, jnp.int32), lax.axis_index("wide"), 0, keepdims=False
    )
    return jnp.concatenate([me[None], row])


def shards(
    tokens,
    lengths,
    cotangent,
    norm_gain,
    conv_weight,
    w_query,
    w_key,
    w_value,
    w_query_window,
    w_key_window,
    w_out,
    ffn_gain,
    w_gate,
    w_up,
    w_down,
    *,
    wide_size,
):
    me = lax.axis_index("grp")
    spot = me * wide_size + lax.axis_index("wide")
    count = tokens.shape[0]
    rows = w_query.shape[0]
    part = w_down.shape[0]
    part_p = -(-part // 16) * 16
    hid_p = wide_size * part_p
    length = lengths[0]
    is_valid = (jnp.arange(count, dtype=jnp.int32) < length).astype(f32)
    table = table_of(wide_size)

    small = jnp.concatenate(
        [
            norm_gain[None],
            conv_weight.T,
            ffn_gain[None],
            jnp.broadcast_to(length.astype(f32), (1, rows)),
            jnp.zeros((2, rows), f32),
        ],
        axis=0,
    ).astype(low)
    small_all = everywhere(small, wide_size)

    half = D // 2
    out_low = w_out.astype(low)
    out_ring = GatherRing([out_low[:, :half], out_low[:, half:]], False, wide_size, table)
    mixer_blocks = split_mixer(table, (w_query, w_key, w_value, w_query_window, w_key_window))
    mixer_got = [mixer_blocks[0]] + [swap(mixer_blocks[r], r) for r in range(1, GROUP)]
    mix_ring = GatherRing(
        [jnp.stack(mixer_got[:2]), jnp.stack(mixer_got[2:])], True, wide_size, table
    )
    gu_blocks = split_gate_up(table, w_gate, w_up, wide_size, part, part_p)
    gu_blocks = after(mixer_got[3], gu_blocks)[0]
    gu_got = [gu_blocks[0]] + [swap(gu_blocks[r], r) for r in range(1, GROUP)]
    gu_ring = GatherRing([jnp.stack(gu_got[:2]), jnp.stack(gu_got[2:])], True, wide_size, table)
    down_low = jnp.pad(w_down.astype(low), ((0, part_p - part), (0, 0)))
    down_ring = GatherRing([down_low[:, :half], down_low[:, half:]], False, wide_size, table)

    g_one, tap_0, tap_1, tap_2, g_two = [
        small_all[:, i].reshape(D).astype(f32) for i in range(5)
    ]
    taps = jnp.stack([tap_0, tap_1, tap_2])
    group_lens = small_all[:, 5, 0].astype(jnp.int32).reshape(GROUP, wide_size)
    group_lens = lax.dynamic_index_in_dim(group_lens, lax.axis_index("wide"), 1, keepdims=False)
    group_lens = reorder(group_lens)

    inputs = tokens.astype(f32)
    conv_out, front_pull = jax.vjp(front_part, inputs, g_one, taps)
    conv_low = group_gather(conv_out.astype(low))
    grad_outer = cotangent.astype(f32) * is_valid[:, None]
    down_own = after(conv_low, grad_outer.astype(low))[0]
    down_in = group_gather(down_own)

    for _ in range(3):
        out_ring.step()
    for k in range(7):
        mix_ring.step()
        out_ring.step()
        if k == 4:
            gu_ring.step(mix_ring.seen())
    gu_ring.step(mix_ring.held[0][-1])
    w_mix = mix_ring.done()
    wo = out_ring.done()

    def advance(token, *rings):
        for ring in rings:
            ring.step(token)

    pack = product(conv_low, w_mix)
    advance(pack, gu_ring)
    mixed = per_sequence(
        mix_kernel, "mix", count, (PACK,), WIN_G, low, group_lens, pack
    )
    advance(mixed, gu_ring)

    def partial_sum(make, between=lambda across: ()):
        far = make(1).astype(low)
        over = swap(far[count:], 1)
        near = make(0).astype(low)
        peer = swap(near[count:], 1)
        across = (far[:count].astype(f32) + over.astype(f32)).astype(low)
        got = swap(across, 2)
        for token in between(across):
            got = after(token, got)[0]
        return near[:count].astype(f32) + peer.astype(f32) + got.astype(f32)

    def rows_of(value, x):
        return value[2 * x * count : 2 * (x + 1) * count]

    def in_forward(across):
        advance(across, gu_ring)
        advance(gu_ring.seen(), gu_ring, down_ring)
        return [gu_ring.seen()]

    resid = inputs + partial_sum(lambda x: product(rows_of(mixed, x), wo), in_forward)
    normed_f, middle_pull = jax.vjp(rms_norm, resid, g_two)
    normed_own = normed_f.astype(low)
    advance(normed_own, gu_ring, down_ring)

    def in_gather():
        down_ring.step(gu_ring.seen())
        return (gu_ring.seen(), down_ring.seen())

    normed = group_gather(normed_own, in_gather)
    w_gu = gu_ring.done(down_ring.seen())
    down_ring.step(w_gu)
    gate_up = product(*after(down_ring.seen(), normed, w_gu))
    advance(gate_up, down_ring)
    gate_pre, up_pre = gate_up[:, :hid_p], gate_up[:, hid_p:]
    sigma = jax.nn.sigmoid(gate_pre)
    silu_gate = gate_pre * sigma
    hidden = bar((silu_gate * up_pre).astype(low))
    advance(hidden, down_ring)

    grad_down = product_tn(*after(down_ring.seen(), hidden, down_in)).astype(low)
    advance(grad_down, down_ring)
    down_sum = SumRing(grad_down.reshape(wide_size, part_p, D), wide_size, table, part)
    down_sum.step()
    down_ring.step(down_sum.last)
    wd = down_ring.done()
    grad_hidden = product_nt(down_in, wd).astype(low).astype(f32)
    grad_gu = jnp.concatenate(
        [
            (grad_hidden * up_pre * sigma * (1.0 + gate_pre * (1.0 - sigma))).astype(low),
            (grad_hidden * silu_gate).astype(low),
        ],
        axis=1,
    )
    grad_gu = bar(grad_gu)
    down_sum.step(grad_gu)
    sums = []

    def in_backward(across):
        down_sum.step(across)
        grad_w_gu = product_tn(*after((across, down_sum.last), normed, grad_gu)).astype(low)
        gu_sum = SumRing(grad_w_gu.reshape(GROUP, wide_size, rows, 2 * hid_p), wide_size, table)
        gu_sum.step()
        down_sum.step(gu_sum.last)
        gu_sum.step(down_sum.last)
        sums.append(gu_sum)
        return [gu_sum.last]

    grad_normed = partial_sum(lambda x: product_nt(rows_of(grad_gu, x), w_gu), in_backward)
    gu_sum = sums[0]
    grad_resid_norm, grad_ffn_gain = middle_pull(grad_normed.astype(low).astype(f32))
    grad_resid = grad_outer + grad_resid_norm
    branch_own = grad_resid.astype(low)
    advance(branch_own, down_sum)

    def in_branch():
        gu_sum.step(down_sum.last)
        return gu_sum.last

    branch_in = group_gather(branch_own, in_branch)
    down_sum.step(branch_in)
    grad_mixed = product_nt(branch_in, wo).astype(low)
    advance(grad_mixed, gu_sum)
    grad_mixed = after(gu_sum.last, grad_mixed)[0]
    grad_pack = per_sequence(
        mix_back_kernel, "mix_back", count, (PACK, WIN_G), PACK, low, group_lens, pack, grad_mixed
    )
    advance(grad_pack, gu_sum)
    grad_w_down = down_sum.done(grad_pack)
    grad_mix = product_tn(*after(gu_sum.last, conv_low, grad_pack)).astype(low)
    mix_sum = SumRing(grad_mix.reshape(GROUP, wide_size, rows, PACK), wide_size, table)
    mix_sum.step()
    advance(mix_sum.last, gu_sum)
    grad_pack = after(gu_sum.last, grad_pack)[0]

    def in_front(across):
        advance(across, mix_sum, gu_sum)
        grad_out = product_tn(*after(gu_sum.last, mixed, branch_in)).astype(low)
        advance(grad_out, mix_sum)
        sums.append(grad_out)
        return [mix_sum.last]

    grad_conv_low = partial_sum(lambda x: product_nt(rows_of(grad_pack, x), w_mix), in_front)
    grad_out = sums[1]
    mix_sum.step(grad_conv_low)
    gu_halves = gu_sum.done(mix_sum.last)
    out_sum = SumRing(grad_out.reshape(wide_size, rows, D), wide_size, table, rows)
    out_sum.step(gu_halves[0])
    grad_conv_low = after(out_sum.last, grad_conv_low)[0]
    grad_front, grad_norm_gain, grad_taps = front_pull(grad_conv_low.astype(low).astype(f32))
    grad_tokens = bar((grad_resid + grad_front).astype(low))
    mix_sum.step(grad_tokens)
    out_sum.step(mix_sum.last)
    out_sum.step()

    def in_down(across):
        mix_sum.step(across)
        out_sum.step(mix_sum.last)
        out_sum.step()
        return [out_sum.last]

    hidden_late = after(out_sum.last, hidden)[0]
    down = partial_sum(lambda x: product(rows_of(hidden_late, x), wd), in_down)
    block_out = bar(((resid + down) * is_valid[:, None]).astype(low))
    mix_sum.step(block_out)
    out_sum.step(mix_sum.last)
    out_sum.step()
    gains = jnp.concatenate(
        [grad_norm_gain[None], grad_taps, grad_ffn_gain[None], jnp.zeros((3, D), f32)], axis=0
    )
    gains = after(out_sum.last, gains)[0]
    seen = []

    def to_owner(halves):
        blocks = [halves[0][0], halves[0][1], halves[1][0], halves[1][1]]
        return [blocks[0]] + [swap(blocks[r], r) for r in range(1, GROUP)]

    gu_blocks = to_owner(after(out_sum.last, *gu_halves))
    mix_blocks = to_owner(mix_sum.done(out_sum.last))
    seen.append(mix_blocks[0])
    grad_w_out = out_sum.done(mix_blocks[0])
    seen.append(grad_w_out)
    grad_gate, grad_up = merge_gate_up(
        table, after(grad_w_out, *gu_blocks), wide_size, part, part_p
    )
    seen.append(grad_gate)
    mixer_grads = merge_mixer(table, after(grad_gate, *mix_blocks))
    seen.append(mixer_grads[0])
    gains = sum_everywhere(gains, wide_size, seen).reshape(8, GROUP * wide_size, rows)
    gains = lax.dynamic_index_in_dim(gains, spot, 1, keepdims=False)
    return (
        block_out,
        grad_tokens,
        gains[0],
        gains[1 : 1 + CONV_K].T,
        *mixer_grads,
        grad_w_out,
        gains[1 + CONV_K],
        grad_gate,
        grad_up,
        grad_w_down,
    )


def solution(mesh):
    rows = P(("grp", "wide"), None)
    flat = P(("grp", "wide"))
    return jax.shard_map(
        functools.partial(shards, wide_size=mesh.shape["wide"]),
        mesh=mesh,
        in_specs=(rows, flat, rows, flat, rows, rows, rows, rows, rows, rows, rows, flat, rows, rows, rows),
        out_specs=(rows, rows, flat, rows, rows, rows, rows, rows, rows, rows, flat, rows, rows, rows),
        check_vma=False,
    )
```

```python
import functools

import jax
import jax.numpy as jnp
from jax import lax
from jax.experimental import pallas as pl
from jax.experimental.pallas import tpu as pltpu
from jax.sharding import PartitionSpec as P

D = 2048
HEADS = 16
FEAT = 16
WINDOW = 64
CONV_K = 3
VHEAD = 128
GROUP = 4
HEADS_G = HEADS // GROUP
LIN_G = HEADS_G * FEAT
WIN_G = HEADS_G * VHEAD
PACK = 2 * LIN_G + 3 * WIN_G

low = jnp.bfloat16
f32 = jnp.float32

CYCLES = {8: (0, 2, 4, 6, 7, 5, 3, 1)}


def dot(left, right, over_left, over_right):
    return lax.dot_general(
        left, right, (((over_left,), (over_right,)), ((), ())), preferred_element_type=f32
    )


def product(left, right):
    return dot(left, right, 1, 0)


def product_tn(left, right):
    return dot(left, right, 0, 0)


def product_nt(left, right):
    return dot(left, right, 1, 1)


def rms_norm(values, gain_vec):
    return values * lax.rsqrt(jnp.mean(values * values, axis=-1, keepdims=True) + 1e-06) * gain_vec


def short_conv(values, taps):
    total = values * taps[0]
    for shift in range(1, CONV_K):
        moved = jnp.concatenate(
            [jnp.zeros((shift, values.shape[1]), f32), values[:-shift]], axis=0
        )
        total = total + moved * taps[shift]
    return total


def front_part(inputs, g_one, taps):
    return short_conv(rms_norm(inputs, g_one), taps)


def head_parts(pack_ref, head, keep, in_window):
    query = pack_ref[:, FEAT * head : FEAT * (head + 1)].astype(low)
    key = pack_ref[:, LIN_G + FEAT * head : LIN_G + FEAT * (head + 1)].astype(low)
    start = 2 * LIN_G + VHEAD * head
    value = pack_ref[:, start : start + VHEAD].astype(low)
    start += WIN_G
    query_win = pack_ref[:, start : start + VHEAD].astype(low)
    start += WIN_G
    key_win = pack_ref[:, start : start + VHEAD].astype(low)
    scores = product_nt(query, key) * FEAT**-0.5
    kernel = jnp.where(keep, 1.0 + scores + 0.5 * scores * scores, 0.0)
    over = 1.0 / jnp.sum(kernel, axis=1, keepdims=True)
    share = kernel * over
    logits = jnp.where(in_window, product_nt(query_win, key_win) * VHEAD**-0.5, -1e30)
    raised = jnp.exp(logits - jnp.max(logits, axis=1, keepdims=True))
    probs = raised * (1.0 / jnp.sum(raised, axis=1, keepdims=True))
    return query, key, value, query_win, key_win, scores, over, share, probs


def masks(length, count):
    row = lax.broadcasted_iota(jnp.int32, (count, count), 0)
    col = lax.broadcasted_iota(jnp.int32, (count, count), 1)
    keep = (row >= col) & (col < length)
    return keep, keep & (row - col < WINDOW)


def mix_kernel(lens_ref, pack_ref, mixed_ref):
    keep, in_window = masks(lens_ref[pl.program_id(0)], pack_ref.shape[0])
    for head in range(HEADS_G):
        parts = head_parts(pack_ref, head, keep, in_window)
        value, share, probs = parts[2], parts[7], parts[8]
        out = product((share + probs).astype(low), value)
        mixed_ref[:, VHEAD * head : VHEAD * (head + 1)] = out.astype(low)


def mix_back_kernel(lens_ref, pack_ref, grad_ref, out_ref):
    keep, in_window = masks(lens_ref[pl.program_id(0)], pack_ref.shape[0])
    grad_query, grad_key = [], []
    for head in range(HEADS_G):
        query, key, value, query_win, key_win, scores, over, share, probs = head_parts(
            pack_ref, head, keep, in_window
        )
        grad = grad_ref[:, VHEAD * head : VHEAD * (head + 1)]
        weights = product_nt(grad, value)
        grad_raw = probs * (weights - jnp.sum(weights * probs, axis=1, keepdims=True))
        grad_raw = (grad_raw * VHEAD**-0.5).astype(low)
        centred = weights - jnp.sum(weights * share, axis=1, keepdims=True)
        grad_scores = jnp.where(keep, centred * (over * FEAT**-0.5) * (1.0 + scores), 0.0)
        grad_scores = grad_scores.astype(low)
        start = 2 * LIN_G + VHEAD * head
        out_ref[:, start : start + VHEAD] = product_tn((share + probs).astype(low), grad).astype(low)
        start += WIN_G
        out_ref[:, start : start + VHEAD] = product(grad_raw, key_win).astype(low)
        start += WIN_G
        out_ref[:, start : start + VHEAD] = product_tn(grad_raw, query_win).astype(low)
        grad_query.append(product(grad_scores, key).astype(low))
        grad_key.append(product_tn(grad_scores, query).astype(low))
    out_ref[:, : 2 * LIN_G] = jnp.concatenate(grad_query + grad_key, axis=1)


def per_sequence(body, name, count, widths, out_width, out_type, lens, *arrays):
    return pl.pallas_call(
        body,
        grid=(GROUP,),
        in_specs=[pl.BlockSpec(memory_space=pltpu.SMEM)]
        + [pl.BlockSpec((count, width), lambda i: (i, 0)) for width in widths],
        out_specs=pl.BlockSpec((count, out_width), lambda i: (i, 0)),
        out_shape=jax.ShapeDtypeStruct((GROUP * count, out_width), out_type),
        compiler_params=pltpu.CompilerParams(vmem_limit_bytes=32 * 1024 * 1024),
        cost_estimate=pl.CostEstimate(
            flops=2_000_000_000, bytes_accessed=10_000_000, transcendentals=1_000_000
        ),
        name=name,
    )(lens, *arrays)


bar = lax.optimization_barrier


def swap(value, over):
    return lax.ppermute(value, "grp", [(i, i ^ over) for i in range(GROUP)])


def group_gather(own, between=lambda: None):
    across = swap(own, 2)
    token = between()
    if token is not None:
        across = after(token, across)[0]
    count = own.shape[0]
    got = swap(jnp.concatenate([own, across]), 1)
    return jnp.concatenate([own, got[:count], across, got[count:]])


def reorder(stack):
    me = lax.axis_index("grp")
    return jnp.concatenate([lax.dynamic_slice_in_dim(stack, me ^ r, 1) for r in range(GROUP)])


def after(token, *values):
    return bar((*values, token))[:-1]


def steps_of(axis, size):
    step = 1
    while step < size:
        yield axis, size, step
        step *= 2


def everywhere(value, wide_size):
    stack = value[None]
    for axis, size, step in list(steps_of("wide", wide_size)) + list(steps_of("grp", GROUP)):
        other = lax.ppermute(stack, axis, [(i, i ^ step) for i in range(size)])
        upper = (lax.axis_index(axis) & step) > 0
        stack = jnp.where(
            upper, jnp.concatenate([other, stack], 0), jnp.concatenate([stack, other], 0)
        )
    return stack


def sum_everywhere(value, wide_size):
    for axis, size, step in list(steps_of("grp", GROUP)) + list(steps_of("wide", wide_size)):
        value = value + lax.ppermute(value, axis, [(i, i ^ step) for i in range(size)])
    return value


SMEM = pl.BlockSpec(memory_space=pltpu.SMEM)
VMEM = pl.BlockSpec(memory_space=pltpu.VMEM)
ANY = pl.BlockSpec(memory_space=pl.ANY)
HBM = pl.BlockSpec(memory_space=pltpu.HBM)


def params(mib):
    return pltpu.CompilerParams(vmem_limit_bytes=mib * 1024 * 1024)


def cost(nbytes, flops=0):
    return pl.CostEstimate(flops=flops, bytes_accessed=nbytes, transcendentals=0)


def split_mixer(table, weights):
    rows = weights[0].shape[0]

    def body(table_ref, *refs):
        out = refs[-1]
        for j in range(GROUP):
            pieces = []
            for ref in refs[:-1]:
                width = ref.shape[1] // GROUP
                pieces.append(ref[:, j * width : (j + 1) * width].astype(low))
            out[j ^ table_ref[0]] = jnp.concatenate(pieces, axis=1)

    return pl.pallas_call(
        body,
        in_specs=[SMEM] + [VMEM] * len(weights),
        out_specs=VMEM,
        out_shape=jax.ShapeDtypeStruct((GROUP, rows, PACK), low),
        compiler_params=params(24),
        cost_estimate=cost(rows * PACK * GROUP * 6),
        name="split_mixer",
    )(table, *weights)


def split_gate_up(table, w_gate, w_up, wide_size, part, part_p):
    rows = w_gate.shape[0]
    hid_p = wide_size * part_p

    def body(table_ref, gate_ref, up_ref, out):
        fill = jnp.zeros((rows, part_p - part), f32)
        for j in range(GROUP):
            pieces = []
            for ref in (gate_ref, up_ref):
                for w in range(wide_size):
                    start = (j * wide_size + w) * part
                    pieces += [ref[:, start : start + part], fill]
            out[j ^ table_ref[0]] = jnp.concatenate(pieces, axis=1).astype(low)

    return pl.pallas_call(
        body,
        in_specs=[SMEM, VMEM, VMEM],
        out_specs=VMEM,
        out_shape=jax.ShapeDtypeStruct((GROUP, rows, 2 * hid_p), low),
        compiler_params=params(24),
        cost_estimate=cost(rows * hid_p * GROUP * 12),
        name="split_gate_up",
    )(table, w_gate, w_up)


def merge_gate_up(table, pieces, wide_size, part, part_p):
    rows = pieces[0].shape[0]
    hid_p = wide_size * part_p
    full = jax.ShapeDtypeStruct((rows, GROUP * wide_size * part), f32)

    def body(table_ref, a, b, c, d, gate_ref, up_ref, held):
        for r, ref in enumerate((a, b, c, d)):
            held[r] = ref[...].astype(f32)
        for at, out in ((0, gate_ref), (hid_p, up_ref)):
            for j in range(GROUP):
                block = held[j ^ table_ref[0]]
                parts = [block[:, at + w * part_p : at + w * part_p + part] for w in range(wide_size)]
                start = j * wide_size * part
                out[:, start : start + wide_size * part] = jnp.concatenate(parts, axis=1)

    return pl.pallas_call(
        body,
        in_specs=[SMEM] + [VMEM] * 4,
        out_specs=[VMEM, VMEM],
        out_shape=[full, full],
        scratch_shapes=[pltpu.VMEM((GROUP, rows, 2 * hid_p), f32)],
        compiler_params=params(24),
        cost_estimate=cost(rows * hid_p * GROUP * 12),
        name="merge_gate_up",
    )(table, *pieces)


def merge_mixer(table, pieces):
    rows = pieces[0].shape[0]
    widths = [LIN_G, LIN_G, WIN_G, WIN_G, WIN_G]

    def body(table_ref, a, b, c, d, *refs):
        outs, held = refs[:-1], refs[-1]
        for r, ref in enumerate((a, b, c, d)):
            held[r] = ref[...].astype(f32)
        blocks = [held[j ^ table_ref[0]] for j in range(GROUP)]
        at = 0
        for width, out in zip(widths, outs):
            out[...] = jnp.concatenate([block[:, at : at + width] for block in blocks], axis=1)
            at += width

    return pl.pallas_call(
        body,
        in_specs=[SMEM] + [VMEM] * 4,
        out_specs=[VMEM] * 5,
        out_shape=[jax.ShapeDtypeStruct((rows, GROUP * width), f32) for width in widths],
        scratch_shapes=[pltpu.VMEM((GROUP, rows, PACK), f32)],
        compiler_params=params(24),
        cost_estimate=cost(rows * PACK * GROUP * 6),
        name="merge_mixer",
    )(table, *pieces)


def place(table, ways, grouped, size):
    piece = ways[0][0]
    rows, width = piece.shape[-2:]
    shape = (GROUP, size, rows, width) if grouped else (size, rows, 2 * width)

    def body(table_ref, *refs):
        out, sems = refs[-2:]
        copies = []
        for d in (0, 1):
            for s in range(size):
                ref = refs[d * size + s]
                owner = table_ref[1 + d * size + s]
                if grouped:
                    for i in range(2):
                        copies.append((ref.at[i], out.at[(2 * d + i) ^ table_ref[0], owner]))
                else:
                    copies.append((ref, out.at[owner, :, d * width : (d + 1) * width]))
        copies = [pltpu.make_async_copy(of, to, sems.at[k]) for k, (of, to) in enumerate(copies)]
        for copy in copies:
            copy.start()
        for copy in copies:
            copy.wait()

    return pl.pallas_call(
        body,
        in_specs=[SMEM] + [ANY if grouped else HBM] * (2 * size),
        out_specs=ANY,
        out_shape=jax.ShapeDtypeStruct(shape, low),
        scratch_shapes=[pltpu.SemaphoreType.DMA(((4 if grouped else 2) * size,))],
        compiler_params=params(2),
        cost_estimate=cost(8 * size * rows * width * piece.ndim),
        name="place",
    )(table, *ways[0], *ways[1])


def pick_add(table, terms, got, step, size, keep_rows=None):
    grouped = terms.ndim == 4
    rows, width = terms.shape[-2:]
    k = (step + 1) % size
    if not grouped:
        width //= 2

    def body(table_ref, *refs):
        mine, outs = refs[:2], refs[-2:] if keep_rows is None else refs[-1:]
        for d in (0, 1):
            total = mine[d][...].reshape(rows, width).astype(f32)
            if got is not None:
                total = total + refs[2 + d][...].reshape(rows, width).astype(f32)
            if keep_rows is None:
                outs[d][...] = total.reshape(outs[d].shape).astype(low)
            else:
                outs[0][:, d * width : (d + 1) * width] = total[:keep_rows]

    def owner(table_ref, d):
        return table_ref[1 + d * size + k]

    if grouped:
        grid = (2,)
        term_specs = [
            pl.BlockSpec(
                (1, 1, rows, width),
                lambda i, t, d=d: ((2 * d + i) ^ t[0], owner(t, d), 0, 0),
            )
            for d in (0, 1)
        ]
        piece = pl.BlockSpec((1, rows, width), lambda i, t: (i, 0, 0))
        shape = jax.ShapeDtypeStruct((2, rows, width), low)
    else:
        grid = (1,)
        term_specs = [
            pl.BlockSpec((1, rows, width), lambda i, t, d=d: (owner(t, d), 0, d)) for d in (0, 1)
        ]
        piece = pl.BlockSpec((rows, width), lambda i, t: (0, 0))
        shape = jax.ShapeDtypeStruct((rows, width), low)
    out_specs, out_shape = [piece, piece], [shape, shape]
    if keep_rows is not None:
        out_specs = [pl.BlockSpec((keep_rows, 2 * width), lambda i, t: (0, 0))]
        out_shape = [jax.ShapeDtypeStruct((keep_rows, 2 * width), f32)]
    came = [] if got is None else list(got)

    return pl.pallas_call(
        body,
        grid_spec=pltpu.PrefetchScalarGridSpec(
            num_scalar_prefetch=1,
            grid=grid,
            in_specs=term_specs + [piece] * len(came),
            out_specs=out_specs,
        ),
        out_shape=out_shape,
        compiler_params=params(16),
        cost_estimate=cost(8 * rows * width * 3),
        name="pick_add",
    )(table, terms, terms, *came)


def round_ring(cycle, d):
    size = len(cycle)
    way = [(cycle[i], cycle[(i + 1) % size]) for i in range(size)]
    return way if d == 0 else [(to, of) for of, to in way]


class GatherRing:
    def __init__(self, halves, grouped, size, table):
        self.held = [[half] for half in halves]
        self.grouped, self.size, self.table = grouped, size, table
        self.steps = size - 1 if size in CYCLES else 0

    def step(self, token=None):
        if self.steps == 0:
            return
        self.steps -= 1
        for d, held in enumerate(self.held):
            value = held[-1] if token is None else after(token, held[-1])[0]
            held.append(lax.ppermute(value, "wide", round_ring(CYCLES[self.size], d)))

    def seen(self):
        return self.held[0][max(len(self.held[0]) - 2, 0)]

    def done(self, token=None):
        while self.steps:
            self.step()
        if self.size in CYCLES:
            ways = self.held
            if token is not None:
                ways = [list(after(token, *held)) for held in ways]
            out = place(self.table, ways, self.grouped, self.size)
        elif self.grouped:
            block = jnp.concatenate([self.held[0][0], self.held[1][0]], axis=0)
            out = jnp.moveaxis(lax.all_gather(block, "wide"), 0, 1)
            out = reorder(out)
        else:
            block = jnp.concatenate([self.held[0][0], self.held[1][0]], axis=1)
            out = lax.all_gather(block, "wide")
        return out.reshape(-1, out.shape[-1])


class SumRing:
    def __init__(self, terms, size, table, keep_rows=None):
        self.terms, self.size, self.table, self.keep_rows = terms, size, table, keep_rows
        self.at, self.got, self.last = 0, None, terms
        self.left = size - 1 if size in CYCLES else 0

    def step(self, token=None):
        if self.left == 0:
            return
        self.left -= 1
        got = self.got
        if token is not None:
            got = after(token, *got) if got is not None else None
            if got is None:
                self.terms = after(token, self.terms)[0]
        sums = pick_add(self.table, self.terms, got, self.at, self.size)
        self.last = sums[0]
        self.at += 1
        cycle = CYCLES[self.size]
        self.got = [lax.ppermute(sums[d], "wide", round_ring(cycle, d)) for d in (0, 1)]

    def done(self, token=None):
        while self.left:
            self.step()
        if self.size in CYCLES:
            got = self.got if token is None else after(token, *self.got)
            out = pick_add(self.table, self.terms, got, self.at, self.size, self.keep_rows)
            return out if self.keep_rows is None else out[0]
        if self.keep_rows is None:
            full = lax.psum_scatter(
                self.terms.astype(f32), "wide", scatter_dimension=1, tiled=True
            )[:, 0]
            full = reorder(full).astype(low)
            return full[:2], full[2:]
        full = lax.psum_scatter(self.terms.astype(f32), "wide", scatter_dimension=0, tiled=True)
        return full[0, : self.keep_rows]


def table_of(wide_size):
    me = lax.axis_index("grp").astype(jnp.int32)
    if wide_size not in CYCLES:
        return me[None]
    cycle = CYCLES[wide_size]
    rows = []
    for w in range(wide_size):
        at = cycle.index(w)
        rows.append(
            [cycle[(at - s) % wide_size] for s in range(wide_size)]
            + [cycle[(at + s) % wide_size] for s in range(wide_size)]
        )
    row = lax.dynamic_index_in_dim(
        jnp.array(rows, jnp.int32), lax.axis_index("wide"), 0, keepdims=False
    )
    return jnp.concatenate([me[None], row])


def shards(
    tokens,
    lengths,
    cotangent,
    norm_gain,
    conv_weight,
    w_query,
    w_key,
    w_value,
    w_query_window,
    w_key_window,
    w_out,
    ffn_gain,
    w_gate,
    w_up,
    w_down,
    *,
    wide_size,
):
    me = lax.axis_index("grp")
    spot = me * wide_size + lax.axis_index("wide")
    count = tokens.shape[0]
    rows = w_query.shape[0]
    part = w_down.shape[0]
    part_p = -(-part // 16) * 16
    hid_p = wide_size * part_p
    length = lengths[0]
    is_valid = (jnp.arange(count, dtype=jnp.int32) < length).astype(f32)
    table = table_of(wide_size)

    small = jnp.concatenate(
        [
            norm_gain[None],
            conv_weight.T,
            ffn_gain[None],
            jnp.broadcast_to(length.astype(f32), (1, rows)),
            jnp.zeros((2, rows), f32),
        ],
        axis=0,
    ).astype(low)
    small_all = everywhere(small, wide_size)

    half = D // 2
    out_low = w_out.astype(low)
    out_ring = GatherRing([out_low[:, :half], out_low[:, half:]], False, wide_size, table)
    mixer_blocks = split_mixer(table, (w_query, w_key, w_value, w_query_window, w_key_window))
    mixer_got = [mixer_blocks[0]] + [swap(mixer_blocks[r], r) for r in range(1, GROUP)]
    mix_ring = GatherRing(
        [jnp.stack(mixer_got[:2]), jnp.stack(mixer_got[2:])], True, wide_size, table
    )
    gu_blocks = split_gate_up(table, w_gate, w_up, wide_size, part, part_p)
    gu_blocks = after(mixer_got[3], gu_blocks)[0]
    gu_got = [gu_blocks[0]] + [swap(gu_blocks[r], r) for r in range(1, GROUP)]
    gu_ring = GatherRing([jnp.stack(gu_got[:2]), jnp.stack(gu_got[2:])], True, wide_size, table)
    down_low = jnp.pad(w_down.astype(low), ((0, part_p - part), (0, 0)))
    down_ring = GatherRing([down_low[:, :half], down_low[:, half:]], False, wide_size, table)

    g_one, tap_0, tap_1, tap_2, g_two = [
        small_all[:, i].reshape(D).astype(f32) for i in range(5)
    ]
    taps = jnp.stack([tap_0, tap_1, tap_2])
    group_lens = small_all[:, 5, 0].astype(jnp.int32).reshape(GROUP, wide_size)
    group_lens = lax.dynamic_index_in_dim(group_lens, lax.axis_index("wide"), 1, keepdims=False)
    group_lens = reorder(group_lens)

    inputs = tokens.astype(f32)
    conv_out, front_pull = jax.vjp(front_part, inputs, g_one, taps)
    conv_low = group_gather(conv_out.astype(low))
    grad_outer = cotangent.astype(f32) * is_valid[:, None]
    down_own = after(conv_low, grad_outer.astype(low))[0]
    down_in = group_gather(down_own)

    for _ in range(3):
        out_ring.step()
    for k in range(7):
        mix_ring.step()
        out_ring.step()
        if k == 4:
            gu_ring.step(mix_ring.seen())
    gu_ring.step(mix_ring.held[0][-1])
    w_mix = mix_ring.done()
    wo = out_ring.done()

    def advance(token, *rings):
        for ring in rings:
            ring.step(token)

    pack = product(conv_low, w_mix)
    advance(pack, gu_ring)
    mixed = per_sequence(
        mix_kernel, "mix", count, (PACK,), WIN_G, low, group_lens, pack
    )
    advance(mixed, gu_ring)

    def partial_sum(make, between=lambda across: ()):
        far = make(1).astype(low)
        over = swap(far[count:], 1)
        near = make(0).astype(low)
        peer = swap(near[count:], 1)
        across = (far[:count].astype(f32) + over.astype(f32)).astype(low)
        got = swap(across, 2)
        for token in between(across):
            got = after(token, got)[0]
        return near[:count].astype(f32) + peer.astype(f32) + got.astype(f32)

    def rows_of(value, x):
        return value[2 * x * count : 2 * (x + 1) * count]

    def in_forward(across):
        advance(across, gu_ring)
        advance(gu_ring.seen(), gu_ring)
        return [gu_ring.seen()]

    resid = inputs + partial_sum(lambda x: product(rows_of(mixed, x), wo), in_forward)
    normed_f, middle_pull = jax.vjp(rms_norm, resid, g_two)
    normed_own = normed_f.astype(low)
    advance(normed_own, gu_ring)

    def in_gather():
        down_ring.step(gu_ring.seen())
        down_ring.step()
        return down_ring.seen()

    normed = group_gather(normed_own, in_gather)
    w_gu = gu_ring.done(down_ring.seen())
    down_ring.step(w_gu)
    gate_up = product(*after(down_ring.seen(), normed, w_gu))
    advance(gate_up, down_ring)
    gate_pre, up_pre = gate_up[:, :hid_p], gate_up[:, hid_p:]
    sigma = jax.nn.sigmoid(gate_pre)
    silu_gate = gate_pre * sigma
    hidden = bar((silu_gate * up_pre).astype(low))
    advance(hidden, down_ring)

    grad_down = product_tn(*after(down_ring.seen(), hidden, down_in)).astype(low)
    advance(grad_down, down_ring)
    down_sum = SumRing(grad_down.reshape(wide_size, part_p, D), wide_size, table, part)
    down_sum.step()
    down_ring.step(down_sum.last)
    wd = down_ring.done()
    grad_hidden = product_nt(down_in, wd).astype(low).astype(f32)
    grad_gu = jnp.concatenate(
        [
            (grad_hidden * up_pre * sigma * (1.0 + gate_pre * (1.0 - sigma))).astype(low),
            (grad_hidden * silu_gate).astype(low),
        ],
        axis=1,
    )
    grad_gu = bar(grad_gu)
    down_sum.step(grad_gu)
    sums = []

    def in_backward(across):
        down_sum.step(across)
        grad_w_gu = product_tn(*after((across, down_sum.last), normed, grad_gu)).astype(low)
        gu_sum = SumRing(grad_w_gu.reshape(GROUP, wide_size, rows, 2 * hid_p), wide_size, table)
        gu_sum.step()
        down_sum.step(gu_sum.last)
        gu_sum.step(down_sum.last)
        sums.append(gu_sum)
        return [gu_sum.last]

    grad_normed = partial_sum(lambda x: product_nt(rows_of(grad_gu, x), w_gu), in_backward)
    gu_sum = sums[0]
    grad_resid_norm, grad_ffn_gain = middle_pull(grad_normed.astype(low).astype(f32))
    grad_resid = grad_outer + grad_resid_norm
    branch_own = grad_resid.astype(low)
    advance(branch_own, down_sum)

    def in_branch():
        gu_sum.step(down_sum.last)
        return gu_sum.last

    branch_in = group_gather(branch_own, in_branch)
    down_sum.step(branch_in)
    grad_mixed = product_nt(branch_in, wo).astype(low)
    advance(grad_mixed, gu_sum)
    grad_mixed = after(gu_sum.last, grad_mixed)[0]
    grad_pack = per_sequence(
        mix_back_kernel, "mix_back", count, (PACK, WIN_G), PACK, low, group_lens, pack, grad_mixed
    )
    advance(grad_pack, gu_sum)
    grad_w_down = down_sum.done(grad_pack)
    grad_mix = product_tn(*after(gu_sum.last, conv_low, grad_pack)).astype(low)
    mix_sum = SumRing(grad_mix.reshape(GROUP, wide_size, rows, PACK), wide_size, table)
    mix_sum.step()
    advance(mix_sum.last, gu_sum)
    grad_pack = after(gu_sum.last, grad_pack)[0]

    def in_front(across):
        advance(across, mix_sum, gu_sum)
        grad_out = product_tn(*after(gu_sum.last, mixed, branch_in)).astype(low)
        advance(grad_out, mix_sum)
        sums.append(grad_out)
        return [mix_sum.last]

    grad_conv_low = partial_sum(lambda x: product_nt(rows_of(grad_pack, x), w_mix), in_front)
    grad_out = sums[1]
    grad_front, grad_norm_gain, grad_taps = front_pull(grad_conv_low.astype(low).astype(f32))
    grad_tokens = (grad_resid + grad_front).astype(low)
    gu_halves = gu_sum.done(mix_sum.last)
    out_sum = SumRing(grad_out.reshape(wide_size, rows, D), wide_size, table, rows)
    out_sum.step(gu_halves[0])
    advance(gu_halves[0], mix_sum)

    def in_down(across):
        advance(across, mix_sum, out_sum)
        return []

    hidden_late = after(gu_halves[0], hidden)[0]
    down = partial_sum(lambda x: product(rows_of(hidden_late, x), wd), in_down)
    block_out = ((resid + down) * is_valid[:, None]).astype(low)

    def to_owner(halves):
        blocks = [halves[0][0], halves[0][1], halves[1][0], halves[1][1]]
        return [blocks[0]] + [swap(blocks[r], r) for r in range(1, GROUP)]

    mix_sum.step()
    out_sum.step()
    grad_gate, grad_up = merge_gate_up(table, to_owner(gu_halves), wide_size, part, part_p)
    advance(grad_gate, mix_sum, out_sum)
    grad_w_out = out_sum.done()
    mixer_grads = merge_mixer(table, to_owner(mix_sum.done()))
    gains = jnp.concatenate(
        [grad_norm_gain[None], grad_taps, grad_ffn_gain[None], jnp.zeros((3, D), f32)], axis=0
    )
    gains = sum_everywhere(gains, wide_size).reshape(8, GROUP * wide_size, rows)
    gains = lax.dynamic_index_in_dim(gains, spot, 1, keepdims=False)
    return (
        block_out,
        grad_tokens,
        gains[0],
        gains[1 : 1 + CONV_K].T,
        *mixer_grads,
        grad_w_out,
        gains[1 + CONV_K],
        grad_gate,
        grad_up,
        grad_w_down,
    )


def solution(mesh):
    rows = P(("grp", "wide"), None)
    flat = P(("grp", "wide"))
    return jax.shard_map(
        functools.partial(shards, wide_size=mesh.shape["wide"]),
        mesh=mesh,
        in_specs=(rows, flat, rows, flat, rows, rows, rows, rows, rows, rows, rows, flat, rows, rows, rows),
        out_specs=(rows, rows, flat, rows, rows, rows, rows, rows, rows, rows, flat, rows, rows, rows),
        check_vma=False,
    )
```
